1024 devices in a mesh: tile: 8 (over x), ens: 64 (over z, y), lev: 2 (over core).
Axes of the slice: x: 8, y: 8, z: 8, core: 2. Of those that a mesh axis runs over, the one named last changes fastest.
Arguments:
- prior_ensemble: bfloat16 [64, 4, 2048, 1024], P('ens', 'lev', 'tile')
- measured_mesh_location: int32 [2, 49152], P('lev', 'tile'), may hold values from 114688 to 524287
- measured_reading: float32 [2, 49152], P('lev', 'tile'), may hold values from -8 to 8
- measured_noise_spread: float32 [2, 49152], P('lev', 'tile'), may hold values from 4 to 16
- ocean_mask: int32 [2048], P('tile'), may hold values from 0 to 1, as said below
- holder_device: int32 [2048], P('tile'), may hold values from 0 to 63, as said below
Outputs:
- analysis: bfloat16 [64, 4, 2048, 1024], P(None, 'lev', ('tile', 'ens'))
The draws below stay inside these ranges and needn't reach their ends.
Inputs may be any that keep to these rules, and one draw needn't show every extreme that they name: `ocean_mask`: wet is 1 for ocean tiles and 0 for land tiles. `holder_device`: in every strip of 256 tiles, each owner holds exactly 4 tiles, ocean or land, and one owner holds 4 ocean tiles.
All inputs are finite; a program needn't handle non-finite values.
Results may differ from the reference program's by a relative error of at most 0.001.
Values may be sent and summed in bfloat16 or wider, within the bound.
A program may use at most 64 MiB of HBM per device.

```python
import math
import jax
import jax.numpy as jnp
from jax import lax

ENSEMBLE_SIZE = 64
TS = 32
TCOLS_DEV = 8
SUBSET_DEPTH_QTY = 2
CAP = 4
NOBS = 6144
PATCHES_IN_SLAB = 256
TROWS = 32
PATCH_POINT_NUM = 1024
STRIPW = 256
ZONE_SLAB_NUMBER = 8
OWNERS = 64
ZONE_PATCH_TALLY = 2048
OVERALL_DEPTHS = 4
OBS = 49152
SLOTS = 2048
N_LEV = 2


def tile_plan(key):
    base = jax.random.fold_in(key, 4041)
    strip_keys = jax.random.split(base, ZONE_SLAB_NUMBER)

    def one_strip(strip_key):
        order = jax.random.permutation(jax.random.fold_in(strip_key, 1), PATCHES_IN_SLAB)
        position = jnp.argsort(order, stable=True).astype(jnp.int32)
        star = jax.random.randint(jax.random.fold_in(strip_key, 2), (), 0, OWNERS)
        coin = jax.random.randint(jax.random.fold_in(strip_key, 3), (PATCHES_IN_SLAB,), 0, 10)
        first = position < CAP
        owners = ((position // CAP + star) % OWNERS).astype(jnp.int32)
        wets = jnp.where(first, 1, (coin < 6).astype(jnp.int32)).astype(jnp.int32)
        return (wets, owners)
    wets, owners = jax.vmap(one_strip)(strip_keys)
    return (wets.reshape(ZONE_PATCH_TALLY), owners.reshape(ZONE_PATCH_TALLY))


def draw_ocean_mask(key, part):
    return tile_plan(key)[0]


def draw_holder_device(key, part):
    return tile_plan(key)[1]


def draw_prior_ensemble(key, part):
    key = jax.random.fold_in(key, 71)
    grid_shape = (ENSEMBLE_SIZE, OVERALL_DEPTHS, ZONE_PATCH_TALLY, PATCH_POINT_NUM)
    noise_part = jax.random.normal(jax.random.fold_in(key, 1), grid_shape, jnp.float32)
    strengths = jnp.array([0.55, 0.3], dtype=jnp.float32)
    members = jax.random.normal(jax.random.fold_in(key, 2), (ENSEMBLE_SIZE, 2), jnp.float32) * strengths[None, :]
    fields = jax.random.normal(jax.random.fold_in(key, 3), (2, OVERALL_DEPTHS, ZONE_PATCH_TALLY, PATCH_POINT_NUM), jnp.float32)
    coherent = members[:, 0, None, None, None] * fields[0][None] + members[:, 1, None, None, None] * fields[1][None]
    return jnp.clip(noise_part + coherent, -6.0, 6.0).astype(jnp.bfloat16)


def draw_measured_mesh_location(key, part):
    key = jax.random.fold_in(key, 93)
    floor_row = min(TROWS * TS // 2, 7 * STRIPW // 4)
    band_rows = TROWS * TS
    grid_shape = (N_LEV, OBS)
    depth_pair = jax.random.randint(jax.random.fold_in(key, 1), grid_shape, 0, SUBSET_DEPTH_QTY, dtype=jnp.int32)
    north_cell = jax.random.randint(jax.random.fold_in(key, 2), grid_shape, floor_row, band_rows, dtype=jnp.int32)
    east_cell = jax.random.randint(jax.random.fold_in(key, 3), grid_shape, 0, STRIPW, dtype=jnp.int32)
    tile_local = north_cell // TS * TCOLS_DEV + east_cell // TS
    cell_local = north_cell % TS * TS + east_cell % TS
    location = depth_pair * (PATCHES_IN_SLAB * PATCH_POINT_NUM) + tile_local * PATCH_POINT_NUM + cell_local
    lowest = floor_row // TS * TCOLS_DEV * PATCH_POINT_NUM + floor_row % TS * TS
    highest = SUBSET_DEPTH_QTY * PATCHES_IN_SLAB * PATCH_POINT_NUM - 1
    location = location.at[0, 0].set(lowest).at[0, 1].set(highest)
    return location.astype(jnp.int32)


def block_levels(stream_key, extent, cuts, low, high):
    level = 1.0
    for dim, shards_of in cuts:
        steps = jax.random.uniform(jax.random.fold_in(jax.random.fold_in(stream_key, 6), dim), (shards_of,), jnp.float32, low / len(cuts), high / len(cuts))
        level = level * jnp.repeat(jnp.exp(steps), extent[dim] // shards_of).reshape((-1,) + (1,) * (len(extent) - 1 - dim))
    return level


def gaussian(key, extent, scale, most, cuts=(), kind=jnp.bfloat16):
    values = scale * jax.random.normal(key, extent, jnp.float32)
    if cuts:
        values = values * block_levels(key, extent, cuts, -0.22, 0.18)
    return jnp.clip(values, -most, most).astype(kind)


def setup_inputs(seed: int = 0) -> dict:
    keys = jax.random.split(jax.random.key(seed), 7)
    prior_ensemble = draw_prior_ensemble(jax.random.fold_in(keys[6], 71), 0)
    measured_mesh_location = draw_measured_mesh_location(jax.random.fold_in(keys[6], 71), 0)
    measured_reading = gaussian(keys[2], (N_LEV, OBS), 2.0, 8.0, ((0, 2), (1, 8)), jnp.float32)
    measured_noise_spread = jnp.clip(jnp.exp(math.log(16.0) - 1.3862944 * jax.random.uniform(keys[3], (N_LEV, OBS), jnp.float32) ** block_levels(keys[3], (N_LEV, OBS), ((0, 2), (1, 8)), -0.2, 0.2)), 4.0, 16.0)
    ocean_mask = draw_ocean_mask(jax.random.fold_in(keys[6], 71), 0)
    holder_device = draw_holder_device(jax.random.fold_in(keys[6], 71), 0)
    return dict(prior_ensemble=prior_ensemble, measured_mesh_location=measured_mesh_location, measured_reading=measured_reading, measured_noise_spread=measured_noise_spread, ocean_mask=ocean_mask, holder_device=holder_device)


def slot_tables(wet_grid, owner_grid):
    slots_all = OWNERS * CAP
    is_wet = wet_grid == 1
    onehot = ((owner_grid[..., None] == jnp.arange(OWNERS, dtype=jnp.int32)) & is_wet[..., None]).astype(jnp.int32)
    before = jnp.cumsum(onehot, axis=-2) - onehot
    ranking = lax.optimization_barrier(jnp.sum(before * onehot, axis=-1))
    slot_of = owner_grid * CAP + ranking
    chosen = (slot_of[..., None, :] == jnp.arange(slots_all, dtype=jnp.int32)[:, None]) & is_wet[..., None, :]
    return chosen.astype(jnp.float32)

def obs_coords(site_index_list, strip_index):
    tile_local = site_index_list // PATCH_POINT_NUM % PATCHES_IN_SLAB
    cell_local = site_index_list % PATCH_POINT_NUM
    latitude = tile_local // TCOLS_DEV * TS + cell_local // TS
    longitude = strip_index * STRIPW + tile_local % TCOLS_DEV * TS + cell_local % TS
    return (latitude.astype(jnp.float32), longitude.astype(jnp.float32))

def reference(prior_ensemble, measured_mesh_location, measured_reading, measured_noise_spread, ocean_mask, holder_device):
    model_mesh = prior_ensemble.reshape(ENSEMBLE_SIZE, N_LEV, SUBSET_DEPTH_QTY, ZONE_SLAB_NUMBER, PATCHES_IN_SLAB, PATCH_POINT_NUM)
    model_mesh = jnp.transpose(model_mesh, (1, 3, 0, 2, 4, 5)).reshape(N_LEV, ZONE_SLAB_NUMBER, ENSEMBLE_SIZE, SUBSET_DEPTH_QTY * PATCHES_IN_SLAB * PATCH_POINT_NUM)
    sites = measured_mesh_location.reshape(N_LEV, ZONE_SLAB_NUMBER, NOBS)
    pick = jax.vmap(jax.vmap(lambda field, position_number: jnp.take(field, position_number, axis=1)))
    ens_obs = pick(model_mesh, sites).astype(jnp.float32)
    strip_ids = jnp.arange(ZONE_SLAB_NUMBER, dtype=jnp.int32)[None, :, None]
    latitude, longitude = obs_coords(sites, strip_ids)
    meta = jnp.stack([measured_reading.reshape(N_LEV, ZONE_SLAB_NUMBER, NOBS), 1.0 / measured_noise_spread.reshape(N_LEV, ZONE_SLAB_NUMBER, NOBS), latitude, longitude], axis=2)
    padded_values = jnp.pad(ens_obs, ((0, 0), (1, 1), (0, 0), (0, 0)))
    padded_meta = jnp.pad(meta, ((0, 0), (1, 1), (0, 0), (0, 0)))
    chosen_all = slot_tables(ocean_mask.reshape(ZONE_SLAB_NUMBER, PATCHES_IN_SLAB), holder_device.reshape(ZONE_SLAB_NUMBER, PATCHES_IN_SLAB))
    prior_slabs = prior_ensemble.reshape(ENSEMBLE_SIZE, OVERALL_DEPTHS, ZONE_SLAB_NUMBER, PATCHES_IN_SLAB, PATCH_POINT_NUM)
    tiles = jnp.arange(PATCHES_IN_SLAB, dtype=jnp.int32)
    centre_lat = (tiles // TCOLS_DEV * TS).astype(jnp.float32) + (TS - 1) / 2.0
    centre_lon_local = (tiles % TCOLS_DEV * TS).astype(jnp.float32) + (TS - 1) / 2.0
    length_sq = (STRIPW / 2.0) ** 2
    eye = jnp.eye(ENSEMBLE_SIZE, dtype=jnp.float32)

    def strip_step(position_number):
        values = lax.dynamic_slice_in_dim(padded_values, position_number, 3, axis=1)
        values = jnp.moveaxis(values, 2, 0).reshape(ENSEMBLE_SIZE, -1)
        info = lax.dynamic_slice_in_dim(padded_meta, position_number, 3, axis=1)
        info = jnp.moveaxis(info, 2, 0).reshape(4, -1)
        mean_obs = lax.optimization_barrier(jnp.mean(values, axis=0))
        deviation = values - mean_obs
        innovation = info[0] - mean_obs
        centre_lon = centre_lon_local + (position_number * STRIPW).astype(jnp.float32)
        dist_sq = (info[2][None, :] - centre_lat[:, None]) ** 2 + (info[3][None, :] - centre_lon[:, None]) ** 2
        weights = jnp.exp(-dist_sq / (2.0 * length_sq)) * info[1][None, :]

        def gram_one(weight_row):
            scaled = deviation * weight_row
            return (jnp.dot(scaled, deviation.T, precision=lax.Precision.HIGHEST), jnp.dot(scaled, innovation, precision=lax.Precision.HIGHEST))
        gram, proj = lax.map(gram_one, weights)
        precision_matrix = (ENSEMBLE_SIZE - 1.0) * eye + gram
        factor = jnp.linalg.cholesky(precision_matrix)
        inv_low = jax.scipy.linalg.solve_triangular(factor, jnp.broadcast_to(eye, factor.shape), lower=True)
        spread = jnp.sqrt(ENSEMBLE_SIZE - 1.0) * jnp.swapaxes(inv_low, 1, 2)
        half = jax.scipy.linalg.solve_triangular(factor, proj[..., None], lower=True)
        mean_weights = jax.scipy.linalg.solve_triangular(factor, half, lower=True, trans=1)[..., 0]
        transform = spread + mean_weights[:, :, None]
        model_vector = lax.dynamic_slice_in_dim(prior_slabs, position_number, 1, axis=2)[:, :, 0].astype(jnp.float32)
        state_mean = lax.optimization_barrier(jnp.mean(model_vector, axis=0))
        tile_analysis = state_mean[None] + jnp.einsum('tmk,mvtc->kvtc', transform, model_vector - state_mean[None], precision=lax.Precision.HIGHEST)
        tile_analysis = tile_analysis.astype(jnp.bfloat16)
        chosen = lax.dynamic_index_in_dim(chosen_all, position_number, 0, keepdims=False).astype(jnp.bfloat16)
        placed = jnp.einsum('pt,kvtc->kvpc', chosen.astype(jnp.float32), tile_analysis.astype(jnp.float32), preferred_element_type=jnp.float32)
        return placed.astype(jnp.bfloat16)
    result = lax.map(strip_step, jnp.arange(ZONE_SLAB_NUMBER, dtype=jnp.int32))
    result = jnp.transpose(result, (1, 2, 0, 3, 4)).reshape(ENSEMBLE_SIZE, OVERALL_DEPTHS, SLOTS, PATCH_POINT_NUM)
    return result
```

```python
import functools
import jax
import jax.numpy as jnp
from jax import lax
from jax.experimental import pallas as pl
from jax.experimental.pallas import tpu as pltpu
from jax.sharding import PartitionSpec as P

TS = 32
CAP = 4
OWNERS = 64
MEMBERS = 64
STRIPS = 8
TILES = 256
CELLS = 1024
STRIPW = 256
ROWS = 48
FIRST_ROW = 112
LENGTH_SQ = (STRIPW / 2.0) ** 2
BLK = 72
MESH = pl.DeviceIdType.MESH
VLIM = 48 * 1024 * 1024


def prep_kernel(prior, idx, mask, holder, vals, outg, coords, fvals):
    strip = lax.axis_index("tile")
    mine = lax.axis_index("ens")
    owner = holder[...]
    wet = mask[...] == 1
    key = jnp.where(wet, owner, -1).astype(jnp.float32)
    key_all = jnp.broadcast_to(key, (TILES, TILES))
    key_t = key_all.T
    earlier = lax.broadcasted_iota(jnp.int32, (TILES, TILES), 0) < lax.broadcasted_iota(
        jnp.int32, (TILES, TILES), 1
    )
    same = (key_all == key_t) & earlier
    rank = jnp.sum(jnp.where(same, 1.0, 0.0), axis=0, keepdims=True).astype(jnp.int32)
    slot = jnp.where(wet, owner * CAP + rank, -1)
    tile = lax.broadcasted_iota(jnp.int32, (1, TILES), 1)
    half = (TS - 1) / 2.0
    clat = (tile // 8 * TS).astype(jnp.float32) + half
    clon = (tile % 8 * TS + strip * STRIPW).astype(jnp.float32) + half
    lats, lons, fills = [], [], []
    for q in range(CAP):
        here = slot == mine * CAP + q
        for into, what in ((lats, clat), (lons, clon), (fills, jnp.ones_like(clat))):
            total = jnp.sum(jnp.where(here, what, 0.0), axis=1, keepdims=True)
            into.append(jnp.broadcast_to(total, (1, 128)))
    coords[...] = jnp.concatenate(lats + lons + fills + fills, axis=0)
    rows = lax.broadcasted_iota(jnp.int32, (OWNERS * 16, 2 * TILES), 0)
    total = None
    for h in range(2):
        target = jnp.concatenate([slot * 4 + h, slot * 4 + 2 + h], axis=1)
        target = jnp.where(jnp.concatenate([wet, wet], axis=1), target, -1)
        pick = jnp.where(rows == target, 1.0, 0.0).astype(jnp.bfloat16)
        part = jnp.dot(
            pick, prior[:, h * 512 : (h + 1) * 512], preferred_element_type=jnp.float32
        )
        total = part if total is None else total + part
    outg[...] = total.astype(jnp.bfloat16).reshape(OWNERS, 16, 512)

    def step(j, carry):
        ids = idx[pl.ds(j * 4, 4), :]
        pieces, highs = [], []
        cell = lax.broadcasted_iota(jnp.int32, (CELLS, 128), 0)
        for i in range(4):
            row = ids[i : i + 1, :]
            pieces.append(jnp.where(cell == (row & (CELLS - 1)), 1.0, 0.0).astype(jnp.bfloat16))
            highs.append((row >> 10) - FIRST_ROW)
        onehot = jnp.concatenate(pieces, axis=1)
        high = jnp.concatenate(highs, axis=1)
        got = jnp.dot(prior[FIRST_ROW:, :], onehot, preferred_element_type=jnp.float32)
        line = lax.broadcasted_iota(jnp.int32, got.shape, 0)
        value = jnp.sum(jnp.where(line == high, got, 0.0), axis=0, keepdims=True)
        for i in range(4):
            fvals[pl.ds(j * 4 + i, 1), :] = value[:, i * 128 : (i + 1) * 128]
        return carry

    lax.fori_loop(0, ROWS // 4, step, 0)
    vals[...] = fvals[...].astype(jnp.bfloat16)


def prep(prior, idx, mask, holder):
    return pl.pallas_call(
        prep_kernel,
        out_shape=(
            jax.ShapeDtypeStruct((ROWS, 128), jnp.bfloat16),
            jax.ShapeDtypeStruct((OWNERS, 16, 512), jnp.bfloat16),
            jax.ShapeDtypeStruct((16, 128), jnp.float32),
        ),
        in_specs=[pl.BlockSpec(memory_space=pltpu.VMEM)] * 4,
        out_specs=[pl.BlockSpec(memory_space=pltpu.VMEM)] * 3,
        scratch_shapes=[pltpu.VMEM((ROWS, 128), jnp.float32)],
        compiler_params=pltpu.CompilerParams(vmem_limit_bytes=VLIM),
        name="prep",
    )(prior, idx, mask, holder)


def weights_into(wscr, idx, noise, tlat, tlon, strip):
    def step(r, carry):
        ids = idx[pl.ds(r, 1), :]
        tile = (ids >> 10) & (TILES - 1)
        cell = ids & (CELLS - 1)
        lat = ((tile >> 3) * TS + (cell >> 5)).astype(jnp.float32)
        lon = (strip * STRIPW + (tile & 7) * TS + (cell & (TS - 1))).astype(jnp.float32)
        dist = (lat - tlat) ** 2 + (lon - tlon) ** 2
        wscr[r] = jnp.exp(-dist / (2.0 * LENGTH_SQ)) * (1.0 / noise[pl.ds(r, 1), :])
        return carry

    lax.fori_loop(0, ROWS, step, 0)


def split(x):
    high = x.astype(jnp.bfloat16)
    low = (x - high.astype(jnp.float32)).astype(jnp.bfloat16)
    return high, low


def gram_steps(fbuf, rows, first, wscr, read, acc):
    def step(k, carry):
        r0 = 2 * k
        x = jnp.concatenate(
            [fbuf[pl.ds(r0 + i, MEMBERS, stride=rows), :] for i in range(2)], axis=1
        )
        mean = jnp.sum(x, axis=0, keepdims=True) * (1.0 / MEMBERS)
        dev = x - mean
        reading = jnp.concatenate([read[pl.ds(first + r0 + i, 1), :] for i in range(2)], axis=1)
        inno = reading - mean
        w = jnp.concatenate([wscr[first + r0], wscr[first + r0 + 1]], axis=1)
        high, low = split(dev)
        right = jnp.concatenate([high, low], axis=0)
        winno = w * inno
        top = lax.broadcasted_iota(jnp.int32, (8, 256), 0) == 0
        blocks = []
        for t in range(12):
            blocks.append(dev * w[t : t + 1, :])
            blocks.append(jnp.where(top, winno[t : t + 1, :], 0.0))
        left = jnp.concatenate(blocks, axis=0)
        lh, ll = split(left)
        dims = (((1,), (1,)), ((), ()))
        acc[...] += lax.dot_general(
            lh, right, dims, preferred_element_type=jnp.float32
        ) + lax.dot_general(ll, right, dims, preferred_element_type=jnp.float32)
        return carry

    lax.fori_loop(0, rows // 2, step, 0)


def main_kernel(
    vals, idx, read, noise, coords, outg, gsum, recv,
    buf_a, buf_b, fa, fb, wscr, cbuf, acc, gp, gr, tot, lr,
    s_own, s_a1, r_a1, s_b1, r_b1, s_a2, r_a2, s_b2, r_b2,
    s_x, r_x, s_c, r_c, s_g, r_g, s_l, r_l,
):
    strip = lax.axis_index("tile")
    ens = lax.axis_index("ens")
    lev = lax.axis_index("lev")
    y, z = ens % 8, ens // 8
    i1, i2 = y + lev * (z - y), z + lev * (y - z)
    n1, n2 = 1 + 7 * lev, 8 - 7 * lev
    low, high = (strip + STRIPS - 1) % STRIPS, (strip + 1) % STRIPS

    barrier = pltpu.get_barrier_semaphore()

    def greet(d, carry):
        pl.semaphore_signal(
            barrier, inc=1, device_id={"ens": (ens + d) % OWNERS}, device_id_type=MESH
        )
        return carry

    lax.fori_loop(1, OWNERS, greet, 0)
    for where in ({"tile": low}, {"tile": high}, {"lev": 1 - lev}):
        pl.semaphore_signal(barrier, inc=1, device_id=where, device_id_type=MESH)
    pl.semaphore_wait(barrier, OWNERS - 1 + 3)

    def send(src, dst, ss, rs, where):
        pltpu.make_async_remote_copy(
            src_ref=src, dst_ref=dst, send_sem=ss, recv_sem=rs, device_id=where,
            device_id_type=MESH,
        ).start()

    def wait_for(ref, sem):
        pltpu.make_async_copy(ref, ref, sem).wait()

    own_a = pltpu.make_async_copy(vals.at[pl.ds(0, 32)], buf_a.at[i2, i1], s_own.at[0])
    own_b = pltpu.make_async_copy(vals.at[pl.ds(32, 16)], buf_b.at[i1, i2], s_own.at[1])
    own_x = pltpu.make_async_copy(outg.at[ens], recv.at[ens], s_own.at[2])
    own_a.start()
    own_b.start()

    send(coords, cbuf.at[1], s_c.at[0], r_c.at[1], {"tile": low})
    send(coords, cbuf.at[0], s_c.at[1], r_c.at[0], {"tile": high})

    def first_a(d, carry):
        p = (i1 + d) % 8
        send(vals.at[pl.ds(0, 32)], buf_a.at[i2, i1], s_a1, r_a1, {"ens": p * n1 + i2 * n2})
        return carry

    def first_b(d, carry):
        p = (i2 + d) % 8
        send(vals.at[pl.ds(32, 16)], buf_b.at[i1, i2], s_b1, r_b1, {"ens": i1 * n1 + p * n2})
        return carry

    def second_a(d, carry):
        p = (i2 + d) % 8
        send(buf_a.at[i2], buf_a.at[i2], s_a2, r_a2, {"ens": i1 * n1 + p * n2})
        return carry

    def second_b(d, carry):
        p = (i1 + d) % 8
        send(buf_b.at[i1], buf_b.at[i1], s_b2, r_b2, {"ens": p * n1 + i2 * n2})
        return carry

    lax.fori_loop(1, 8, first_a, 0)
    lax.fori_loop(1, 8, first_b, 0)
    own_a.wait()
    wait_for(buf_a.at[0, pl.ds(0, 7)], r_a1)
    lax.fori_loop(1, 8, second_a, 0)
    own_b.wait()
    wait_for(buf_b.at[0, pl.ds(0, 7)], r_b1)
    lax.fori_loop(1, 8, second_b, 0)

    own_x.start()

    def exchange(d, carry):
        other = (ens + d) % OWNERS
        send(outg.at[other], recv.at[ens], s_x, r_x, {"ens": other})
        return carry

    lax.fori_loop(1, OWNERS, exchange, 0)

    wait_for(cbuf.at[0], r_c.at[0])
    wait_for(cbuf.at[1], r_c.at[1])
    pad = jnp.zeros((4, 128), jnp.float32)
    tlat = jnp.concatenate([cbuf[0, 0:4], coords[0:4], cbuf[1, 0:4], pad], axis=0)
    tlon = jnp.concatenate([cbuf[0, 4:8], coords[4:8], cbuf[1, 4:8], pad], axis=0)
    weights_into(wscr, idx, noise, tlat, tlon, strip)
    acc[...] = jnp.zeros_like(acc)

    wait_for(buf_b.at[pl.ds(0, 7)], r_b2)

    def widen_b(k, carry):
        a, b = k // 8, k % 8
        m = a * n1 + b * n2
        fb[pl.ds(pl.multiple_of(m * 16, 16), 16), :] = buf_b[a, b].astype(jnp.float32)
        return carry

    lax.fori_loop(0, MEMBERS, widen_b, 0)
    gram_steps(fb, 16, 32, wscr, read, acc)

    wait_for(buf_a.at[pl.ds(0, 7)], r_a2)

    def widen_a(k, carry):
        a, b = k // 8, k % 8
        m = b * n1 + a * n2
        fa[pl.ds(pl.multiple_of(m * 32, 32), 32), :] = buf_a[a, b].astype(jnp.float32)
        return carry

    lax.fori_loop(0, MEMBERS, widen_a, 0)
    gram_steps(fa, 32, 0, wscr, read, acc)

    for g in range(3):
        for p in range(2):
            sides = []
            for q in range(2):
                t = g * 4 + p * 2 + q
                block = acc[t * BLK : (t + 1) * BLK, :]
                sides.append(block[:, :64] + block[:, 64:])
            gp[g, p] = jnp.concatenate(sides, axis=1)
    send(gp.at[0], gr.at[1], s_g.at[0], r_g.at[1], {"tile": low})
    send(gp.at[2], gr.at[0], s_g.at[1], r_g.at[0], {"tile": high})
    wait_for(gr.at[0], r_g.at[0])
    wait_for(gr.at[1], r_g.at[1])
    tot[...] = (
        gp[1]
        + jnp.where(strip > 0, gr[0], jnp.zeros_like(gr[0]))
        + jnp.where(strip < STRIPS - 1, gr[1], jnp.zeros_like(gr[1]))
    )
    send(tot, lr, s_l, r_l, {"lev": 1 - lev})
    wait_for(lr, r_l)
    gsum[...] = tot[...] + lr[...]

    own_x.wait()
    wait_for(recv.at[pl.ds(0, OWNERS - 1)], r_x)
    wait_for(outg.at[pl.ds(0, OWNERS - 1)], s_x)
    wait_for(buf_a.at[0, pl.ds(0, 7)], s_a1)
    wait_for(buf_b.at[0, pl.ds(0, 7)], s_b1)
    wait_for(buf_a.at[pl.ds(0, 7)], s_a2)
    wait_for(buf_b.at[pl.ds(0, 7)], s_b2)
    for i in range(2):
        wait_for(coords, s_c.at[i])
        wait_for(gp.at[0], s_g.at[i])
    wait_for(tot, s_l)


def spread_out(vals, idx, read, noise, coords, outg):
    dma = pltpu.SemaphoreType.DMA
    vmem = pl.BlockSpec(memory_space=pltpu.VMEM)
    any_ = pl.BlockSpec(memory_space=pl.ANY)
    return pl.pallas_call(
        main_kernel,
        out_shape=(
            jax.ShapeDtypeStruct((2, BLK, 128), jnp.float32),
            jax.ShapeDtypeStruct((MEMBERS, 16, 512), jnp.bfloat16),
        ),
        in_specs=[vmem] * 5 + [any_],
        out_specs=[vmem, any_],
        scratch_shapes=[
            pltpu.VMEM((8, 8, 32, 128), jnp.bfloat16),
            pltpu.VMEM((8, 8, 16, 128), jnp.bfloat16),
            pltpu.VMEM((MEMBERS * 32, 128), jnp.float32),
            pltpu.VMEM((MEMBERS * 16, 128), jnp.float32),
            pltpu.VMEM((ROWS, 16, 128), jnp.float32),
            pltpu.VMEM((2, 16, 128), jnp.float32),
            pltpu.VMEM((12 * BLK, 128), jnp.float32),
            pltpu.VMEM((3, 2, BLK, 128), jnp.float32),
            pltpu.VMEM((2, 2, BLK, 128), jnp.float32),
            pltpu.VMEM((2, BLK, 128), jnp.float32),
            pltpu.VMEM((2, BLK, 128), jnp.float32),
            dma((3,)),
            dma, dma, dma, dma, dma, dma, dma, dma,
            dma, dma,
            dma((2,)), dma((2,)), dma((2,)), dma((2,)),
            dma, dma,
        ],
        compiler_params=pltpu.CompilerParams(
            collective_id=1, has_side_effects=True, vmem_limit_bytes=VLIM
        ),
        name="spread",
    )(vals, idx, read, noise, coords, outg)


def finish_kernel(gsum, coords, recv, out, wide, res):
    for c in range(4):
        wide[c] = recv[:, :, c * 128 : (c + 1) * 128].astype(jnp.float32).reshape(-1, 128)
    row = lax.broadcasted_iota(jnp.int32, (MEMBERS, 128), 0)
    lane = lax.broadcasted_iota(jnp.int32, (MEMBERS, 128), 1)
    eye = row == lane
    eye_r = row + MEMBERS == lane
    mats, projs = [], []
    for q in range(CAP):
        pair = gsum[q // 2]
        if q % 2:
            pair = jnp.concatenate([pair[:, 64:], pair[:, :64]], axis=1)
        body = pair[:64] + jnp.where(eye, MEMBERS - 1.0, 0.0)
        mats.append(jnp.where(lane < 64, body, jnp.where(eye_r, 1.0, 0.0)))
        projs.append(pair[64:65])
    mats = [[m[8 * v : 8 * v + 8] for v in range(8)] for m in mats]
    sub = lax.broadcasted_iota(jnp.int32, (8, 128), 0)
    for j in range(MEMBERS):
        v0, r = j // 8, j % 8
        for q in range(CAP):
            m = mats[q]
            prow = m[v0][r : r + 1, :]
            piv = prow[:, j : j + 1]
            scaled = prow / piv
            for v in range(v0, 8):
                col = m[v][:, j : j + 1]
                if v == v0:
                    if r == 7:
                        continue
                    col = jnp.where(sub[:, :1] > r, col, 0.0)
                m[v] = m[v] - col * scaled
    for q in range(CAP):
        m = jnp.concatenate(mats[q], axis=0)
        diag = jnp.sum(jnp.where(eye, m, 0.0), axis=1, keepdims=True)
        inv = m[:, 64:] * lax.rsqrt(diag)
        proj = projs[q][:, :64]
        zed = jnp.sum(inv * proj, axis=1, keepdims=True)
        mean_w = jnp.sum(inv * zed, axis=0, keepdims=True)
        trans = inv * (MEMBERS - 1.0) ** 0.5 + mean_w
        trans = trans + (1.0 - jnp.sum(trans, axis=1, keepdims=True)) * (1.0 / MEMBERS)
        trans = trans * coords[8 + q : 9 + q, :64]
        t0 = trans.astype(jnp.bfloat16)
        rest = trans - t0.astype(jnp.float32)
        t1, t2 = split(rest)
        left = jnp.concatenate([t0, t1, t2], axis=0)
        for v in range(2):
            for h in range(2):
                r = q * 4 + v * 2 + h
                x = jnp.concatenate(
                    [wide[c, pl.ds(r, MEMBERS, stride=16), :] for c in range(4)], axis=1
                ).astype(jnp.bfloat16)
                got = jnp.dot(left, x, preferred_element_type=jnp.float32)
                got = got[:64] + (got[64:128] + got[128:])
                for c in range(4):
                    res[h * 4 + c, pl.ds(v * 4 + q, MEMBERS, stride=8), :] = got[
                        :, c * 128 : (c + 1) * 128
                    ]
    for c in range(8):
        body = res[c].reshape(MEMBERS, 2, CAP, 128).astype(jnp.bfloat16)
        out[:, :, :, c * 128 : (c + 1) * 128] = body


def finish(gsum, coords, recv):
    return pl.pallas_call(
        finish_kernel,
        out_shape=jax.ShapeDtypeStruct((MEMBERS, 2, CAP, CELLS), jnp.bfloat16),
        in_specs=[pl.BlockSpec(memory_space=pltpu.VMEM)] * 3,
        out_specs=pl.BlockSpec(memory_space=pltpu.VMEM),
        scratch_shapes=[
            pltpu.VMEM((4, MEMBERS * 16, 128), jnp.float32),
            pltpu.VMEM((8, MEMBERS * 8, 128), jnp.float32),
        ],
        compiler_params=pltpu.CompilerParams(vmem_limit_bytes=VLIM),
        name="finish",
    )(gsum, coords, recv)


def local(prior, location, reading, noise, ocean, holder):
    prior = prior.reshape(2 * TILES, CELLS)
    idx = location.reshape(ROWS, 128)
    read = reading.reshape(ROWS, 128)
    spread = noise.reshape(ROWS, 128)
    vals, outg, coords = prep(prior, idx, ocean.reshape(1, TILES), holder.reshape(1, TILES))
    gsum, recv = spread_out(vals, idx, read, spread, coords, outg)
    return finish(gsum, coords, recv)


def solution(mesh):
    in_specs = (
        P("ens", "lev", "tile", None),
        P("lev", "tile"),
        P("lev", "tile"),
        P("lev", "tile"),
        P("tile"),
        P("tile"),
    )
    out_specs = P(None, "lev", ("tile", "ens"), None)
    return jax.shard_map(local, mesh=mesh, in_specs=in_specs, out_specs=out_specs, check_vma=False)
```

```python
import functools
import jax
import jax.numpy as jnp
from jax import lax
from jax.experimental import pallas as pl
from jax.experimental.pallas import tpu as pltpu
from jax.sharding import PartitionSpec as P

TS = 32
CAP = 4
OWNERS = 64
MEMBERS = 64
TILES = 256
CELLS = 1024
STRIPW = 256
ROWS = 48
FIRST_ROW = 112
LENGTH_SQ = (STRIPW / 2.0) ** 2
BLK = 72
EARLY = 8
MESH = pl.DeviceIdType.MESH
VLIM = 56 * 1024 * 1024


def pick_tiles(prior, mask, holder, outg, coords, strip, mine):
    owner = holder[...]
    wet = mask[...] == 1
    key = jnp.where(wet, owner, -1).astype(jnp.float32)
    key_all = jnp.broadcast_to(key, (TILES, TILES))
    key_t = key_all.T
    earlier = lax.broadcasted_iota(jnp.int32, (TILES, TILES), 0) < lax.broadcasted_iota(
        jnp.int32, (TILES, TILES), 1
    )
    same = (key_all == key_t) & earlier
    rank = jnp.sum(jnp.where(same, 1.0, 0.0), axis=0, keepdims=True).astype(jnp.int32)
    slot = jnp.where(wet, owner * CAP + rank, -1)
    tile = lax.broadcasted_iota(jnp.int32, (1, TILES), 1)
    half = (TS - 1) / 2.0
    clat = (tile // 8 * TS).astype(jnp.float32) + half
    clon = (tile % 8 * TS + strip * STRIPW).astype(jnp.float32) + half
    lats, lons, fills = [], [], []
    for q in range(CAP):
        here = slot == mine * CAP + q
        for into, what in ((lats, clat), (lons, clon), (fills, jnp.ones_like(clat))):
            total = jnp.sum(jnp.where(here, what, 0.0), axis=1, keepdims=True)
            into.append(jnp.broadcast_to(total, (1, 128)))
    coords[...] = jnp.concatenate(lats + lons + fills + fills, axis=0)
    rows = lax.broadcasted_iota(jnp.int32, (OWNERS * 16, 2 * TILES), 0)
    total = None
    for h in range(2):
        target = jnp.concatenate([slot * 4 + h, slot * 4 + 2 + h], axis=1)
        target = jnp.where(jnp.concatenate([wet, wet], axis=1), target, -1)
        pick = jnp.where(rows == target, 1.0, 0.0).astype(jnp.bfloat16)
        part = jnp.dot(
            pick, prior[:, h * 512 : (h + 1) * 512], preferred_element_type=jnp.float32
        )
        total = part if total is None else total + part
    outg[...] = total.astype(jnp.bfloat16).reshape(OWNERS, 16, 512)


def gather_rows(prior, idx, fvals, first, count):
    def step(j, carry):
        base = first + j * 4
        pieces, highs = [], []
        cell = lax.broadcasted_iota(jnp.int32, (CELLS, 128), 0)
        for i in range(4):
            row = idx[pl.ds(base + i, 1), :]
            pieces.append(jnp.where(cell == (row & (CELLS - 1)), 1.0, 0.0).astype(jnp.bfloat16))
            highs.append((row >> 10) - FIRST_ROW)
        onehot = jnp.concatenate(pieces, axis=1)
        high = jnp.concatenate(highs, axis=1)
        got = jnp.dot(prior[FIRST_ROW:, :], onehot, preferred_element_type=jnp.float32)
        line = lax.broadcasted_iota(jnp.int32, got.shape, 0)
        value = jnp.sum(jnp.where(line == high, got, 0.0), axis=0, keepdims=True)
        for i in range(4):
            fvals[pl.ds(base + i, 1), :] = value[:, i * 128 : (i + 1) * 128]
        return carry

    lax.fori_loop(0, count // 4, step, 0)


def weights_into(wscr, idx, noise, tlat, tlon, strip):
    def step(r, carry):
        ids = idx[pl.ds(r, 1), :]
        tile = (ids >> 10) & (TILES - 1)
        cell = ids & (CELLS - 1)
        lat = ((tile >> 3) * TS + (cell >> 5)).astype(jnp.float32)
        lon = (strip * STRIPW + (tile & 7) * TS + (cell & (TS - 1))).astype(jnp.float32)
        dist = (lat - tlat) ** 2 + (lon - tlon) ** 2
        wscr[r] = jnp.exp(-dist / (2.0 * LENGTH_SQ)) * (1.0 / noise[pl.ds(r, 1), :])
        return carry

    lax.fori_loop(0, ROWS, step, 0)


def split(x):
    high = x.astype(jnp.bfloat16)
    low = (x - high.astype(jnp.float32)).astype(jnp.bfloat16)
    return high, low


def gram_steps(fbuf, rows, first, wscr, read, acc):
    count = 8

    def step(k, carry):
        r0 = count * k
        take = range(count)
        x = jnp.concatenate(
            [fbuf[pl.ds(r0 + i, MEMBERS, stride=rows), :] for i in take], axis=1
        )
        mean = jnp.sum(x, axis=0, keepdims=True) * (1.0 / MEMBERS)
        dev = x - mean
        reading = jnp.concatenate([read[pl.ds(first + r0 + i, 1), :] for i in take], axis=1)
        inno = reading - mean
        w = jnp.concatenate([wscr[first + r0 + i] for i in take], axis=1)
        high, low = split(dev)
        right = jnp.concatenate([high, low], axis=0)
        left = jnp.concatenate([dev * w[t : t + 1, :] for t in range(12)] + [w * inno], axis=0)
        lh, ll = split(left)
        dims = (((1,), (1,)), ((), ()))
        acc[...] += lax.dot_general(
            lh, right, dims, preferred_element_type=jnp.float32
        ) + lax.dot_general(ll, right, dims, preferred_element_type=jnp.float32)
        return carry

    lax.fori_loop(0, rows // count, step, 0)


def main_kernel(
    prior_in, idx_in, mask_in, holder_in, read_in, noise_in, gsum, recv, coords,
    prior, idx, mask, holder, read, noise, s_in, outg, vals, fvals, buf_a, buf_b, fa, fb, wscr, cown, cbuf, acc, gp, gr, tot, lr,
    s_own, s_a1, r_a1, s_b1, r_b1, s_a2, r_a2, s_b2, r_b2,
    s_x, r_x, s_c, r_c, s_g, r_g, s_l, r_l,
):
    strips = lax.axis_size("tile")
    strip = lax.axis_index("tile")
    ens = lax.axis_index("ens")
    lev = lax.axis_index("lev")
    y, z = ens % 8, ens // 8
    i1, i2 = y + lev * (z - y), z + lev * (y - z)
    n1, n2 = 1 + 7 * lev, 8 - 7 * lev
    low, high = (strip + strips - 1) % strips, (strip + 1) % strips
    sign = 1 - 2 * lev

    loads = [
        pltpu.make_async_copy(src, dst, s_in.at[i])
        for i, (src, dst) in enumerate(
            (
                (mask_in, mask), (holder_in, holder), (prior_in, prior),
                (idx_in, idx), (read_in, read), (noise_in, noise),
            )
        )
    ]
    for load in loads:
        load.start()
    barrier = pltpu.get_barrier_semaphore()

    def greet(d, carry):
        pl.semaphore_signal(
            barrier, inc=1, device_id={"ens": (ens + d) % OWNERS}, device_id_type=MESH
        )
        return carry

    lax.fori_loop(1, OWNERS, greet, 0)
    for where in ({"tile": low}, {"tile": high}, {"lev": 1 - lev}):
        pl.semaphore_signal(barrier, inc=1, device_id=where, device_id_type=MESH)

    for load in loads:
        load.wait()
    pick_tiles(prior, mask, holder, outg, cown, strip, ens)
    coords[...] = cown[...]
    pl.semaphore_wait(barrier, OWNERS - 1 + 3)

    def send(src, dst, ss, rs, where):
        pltpu.make_async_remote_copy(
            src_ref=src, dst_ref=dst, send_sem=ss, recv_sem=rs, device_id=where,
            device_id_type=MESH,
        ).start()

    def wait_for(ref, sem):
        pltpu.make_async_copy(ref, ref, sem).wait()

    def to(dy, dz):
        other = (y + sign * dy + 16) % 8 + 8 * ((z + sign * dz + 16) % 8)
        send(outg.at[other], recv.at[ens], s_x, r_x, {"ens": other})

    def turn(k, carry):
        u, v = 1 + k // 4, k % 4
        to(u, v)
        to(-v, u)
        to(-u, -v)
        to(v, -u)
        return carry

    own_x = pltpu.make_async_copy(outg.at[ens], recv.at[ens], s_own.at[2])
    own_x.start()
    send(cown, cbuf.at[1], s_c.at[0], r_c.at[1], {"tile": low})
    send(cown, cbuf.at[0], s_c.at[1], r_c.at[0], {"tile": high})
    lax.fori_loop(0, EARLY, turn, 0)

    own_a = pltpu.make_async_copy(vals.at[pl.ds(0, 32)], buf_a.at[i2, i1], s_own.at[0])
    own_b = pltpu.make_async_copy(vals.at[pl.ds(32, 16)], buf_b.at[i1, i2], s_own.at[1])

    def first_a(d, carry):
        p = (i1 + d) % 8
        send(vals.at[pl.ds(0, 32)], buf_a.at[i2, i1], s_a1, r_a1, {"ens": p * n1 + i2 * n2})
        return carry

    def first_b(d, carry):
        p = (i2 + d) % 8
        send(vals.at[pl.ds(32, 16)], buf_b.at[i1, i2], s_b1, r_b1, {"ens": i1 * n1 + p * n2})
        return carry

    def second_a(d, carry):
        p = (i2 + d) % 8
        send(buf_a.at[i2], buf_a.at[i2], s_a2, r_a2, {"ens": i1 * n1 + p * n2})
        return carry

    def second_b(d, carry):
        p = (i1 + d) % 8
        send(buf_b.at[i1], buf_b.at[i1], s_b2, r_b2, {"ens": p * n1 + i2 * n2})
        return carry

    gather_rows(prior, idx, fvals, 32, 16)
    vals[32:48] = fvals[32:48].astype(jnp.bfloat16)
    own_b.start()
    lax.fori_loop(1, 8, first_b, 0)
    gather_rows(prior, idx, fvals, 0, 32)
    vals[0:32] = fvals[0:32].astype(jnp.bfloat16)
    own_a.start()
    lax.fori_loop(1, 8, first_a, 0)
    own_b.wait()
    wait_for(buf_b.at[0, pl.ds(0, 7)], r_b1)
    lax.fori_loop(1, 8, second_b, 0)

    wait_for(cbuf.at[0], r_c.at[0])
    wait_for(cbuf.at[1], r_c.at[1])
    pad = jnp.zeros((4, 128), jnp.float32)
    tlat = jnp.concatenate([cbuf[0, 0:4], cown[0:4], cbuf[1, 0:4], pad], axis=0)
    tlon = jnp.concatenate([cbuf[0, 4:8], cown[4:8], cbuf[1, 4:8], pad], axis=0)
    weights_into(wscr, idx, noise, tlat, tlon, strip)
    acc[...] = jnp.zeros_like(acc)

    own_a.wait()
    wait_for(buf_a.at[0, pl.ds(0, 7)], r_a1)
    lax.fori_loop(1, 8, second_a, 0)

    lax.fori_loop(EARLY, 12, turn, 0)
    lax.fori_loop(13, 16, turn, 0)
    to(4, 4)
    to(4, 0)
    to(0, 4)

    wait_for(buf_b.at[pl.ds(0, 7)], r_b2)

    def widen_b(k, carry):
        a, b = k // 8, k % 8
        m = a * n1 + b * n2
        fb[pl.ds(pl.multiple_of(m * 16, 16), 16), :] = buf_b[a, b].astype(jnp.float32)
        return carry

    lax.fori_loop(0, MEMBERS, widen_b, 0)
    gram_steps(fb, 16, 32, wscr, read, acc)

    wait_for(buf_a.at[pl.ds(0, 7)], r_a2)

    def widen_a(k, carry):
        a, b = k // 8, k % 8
        m = b * n1 + a * n2
        fa[pl.ds(pl.multiple_of(m * 32, 32), 32), :] = buf_a[a, b].astype(jnp.float32)
        return carry

    lax.fori_loop(0, MEMBERS, widen_a, 0)
    gram_steps(fa, 32, 0, wscr, read, acc)

    pad = jnp.zeros((6, 128), jnp.float32)
    for g in range(3):
        for p in range(2):
            sides, tails = [], []
            for q in range(2):
                t = g * 4 + p * 2 + q
                block = acc[t * MEMBERS : (t + 1) * MEMBERS, :]
                sides.append(block[:, :64] + block[:, 64:])
                line = acc[12 * MEMBERS + t : 12 * MEMBERS + t + 1, :]
                tails.append(line[:, :64] + line[:, 64:])
            gp[g, p, 0:64] = jnp.concatenate(sides, axis=1)
            gp[g, p, 64:BLK] = jnp.broadcast_to(jnp.concatenate(tails, axis=1), (8, 128))
    send(gp.at[0], gr.at[1], s_g.at[0], r_g.at[1], {"tile": low})
    send(gp.at[2], gr.at[0], s_g.at[1], r_g.at[0], {"tile": high})
    wait_for(gr.at[0], r_g.at[0])
    wait_for(gr.at[1], r_g.at[1])
    tot[...] = (
        gp[1]
        + jnp.where(strip > 0, gr[0], jnp.zeros_like(gr[0]))
        + jnp.where(strip < strips - 1, gr[1], jnp.zeros_like(gr[1]))
    )
    send(tot, lr, s_l, r_l, {"lev": 1 - lev})
    wait_for(lr, r_l)
    gsum[...] = tot[...] + lr[...]

    own_x.wait()
    wait_for(recv.at[pl.ds(0, OWNERS - 1)], r_x)
    wait_for(outg.at[pl.ds(0, OWNERS - 1)], s_x)
    wait_for(buf_a.at[0, pl.ds(0, 7)], s_a1)
    wait_for(buf_b.at[0, pl.ds(0, 7)], s_b1)
    wait_for(buf_a.at[pl.ds(0, 7)], s_a2)
    wait_for(buf_b.at[pl.ds(0, 7)], s_b2)
    for i in range(2):
        wait_for(cown, s_c.at[i])
        wait_for(gp.at[0], s_g.at[i])
    wait_for(tot, s_l)


def spread_out(prior, idx, mask, holder, read, noise):
    dma = pltpu.SemaphoreType.DMA
    vmem = pl.BlockSpec(memory_space=pltpu.VMEM)
    any_ = pl.BlockSpec(memory_space=pl.ANY)
    return pl.pallas_call(
        main_kernel,
        out_shape=(
            jax.ShapeDtypeStruct((2, BLK, 128), jnp.float32),
            jax.ShapeDtypeStruct((MEMBERS, 16, 512), jnp.bfloat16),
            jax.ShapeDtypeStruct((16, 128), jnp.float32),
        ),
        in_specs=[any_] * 6,
        out_specs=[vmem, any_, vmem],
        scratch_shapes=[
            pltpu.VMEM((2 * TILES, CELLS), jnp.bfloat16),
            pltpu.VMEM((ROWS, 128), jnp.int32),
            pltpu.VMEM((1, TILES), jnp.int32),
            pltpu.VMEM((1, TILES), jnp.int32),
            pltpu.VMEM((ROWS, 128), jnp.float32),
            pltpu.VMEM((ROWS, 128), jnp.float32),
            dma((6,)),
            pltpu.VMEM((OWNERS, 16, 512), jnp.bfloat16),
            pltpu.VMEM((ROWS, 128), jnp.bfloat16),
            pltpu.VMEM((ROWS, 128), jnp.float32),
            pltpu.VMEM((8, 8, 32, 128), jnp.bfloat16),
            pltpu.VMEM((8, 8, 16, 128), jnp.bfloat16),
            pltpu.VMEM((MEMBERS * 32, 128), jnp.float32),
            pltpu.VMEM((MEMBERS * 16, 128), jnp.float32),
            pltpu.VMEM((ROWS, 16, 128), jnp.float32),
            pltpu.VMEM((16, 128), jnp.float32),
            pltpu.VMEM((2, 16, 128), jnp.float32),
            pltpu.VMEM((12 * MEMBERS + 16, 128), jnp.float32),
            pltpu.VMEM((3, 2, BLK, 128), jnp.float32),
            pltpu.VMEM((2, 2, BLK, 128), jnp.float32),
            pltpu.VMEM((2, BLK, 128), jnp.float32),
            pltpu.VMEM((2, BLK, 128), jnp.float32),
            dma((3,)),
            dma, dma, dma, dma, dma, dma, dma, dma,
            dma, dma,
            dma((2,)), dma((2,)), dma((2,)), dma((2,)),
            dma, dma,
        ],
        compiler_params=pltpu.CompilerParams(
            collective_id=1, has_side_effects=True, vmem_limit_bytes=VLIM
        ),
        name="spread",
    )(prior, idx, mask, holder, read, noise)


def finish_kernel(gsum, coords, recv, out, wide, res):
    for c in range(4):
        wide[c] = recv[:, :, c * 128 : (c + 1) * 128].astype(jnp.float32).reshape(-1, 128)
    row = lax.broadcasted_iota(jnp.int32, (MEMBERS, 128), 0)
    lane = lax.broadcasted_iota(jnp.int32, (MEMBERS, 128), 1)
    eye = row == lane
    eye_r = row + MEMBERS == lane
    mats, projs = [], []
    for q in range(CAP):
        pair = gsum[q // 2]
        if q % 2:
            pair = jnp.concatenate([pair[:, 64:], pair[:, :64]], axis=1)
        body = pair[:64] + jnp.where(eye, MEMBERS - 1.0, 0.0)
        mats.append(jnp.where(lane < 64, body, jnp.where(eye_r, 1.0, 0.0)))
        projs.append(pair[64:65])
    mats = [[m[8 * v : 8 * v + 8] for v in range(8)] for m in mats]
    sub = lax.broadcasted_iota(jnp.int32, (8, 128), 0)
    for j in range(0, MEMBERS, 2):
        v0, r = j // 8, j % 8
        for q in range(CAP):
            m = mats[q]
            ra, rb = m[v0][r : r + 1, :], m[v0][r + 1 : r + 2, :]
            pa = jnp.broadcast_to(ra[:, j : j + 1], (1, 128))
            pb = jnp.broadcast_to(ra[:, j + 1 : j + 2], (1, 128))
            pc = jnp.broadcast_to(rb[:, j + 1 : j + 2], (1, 128))
            inv = 1.0 / pa
            ratio = pb * inv
            sa = ra * inv
            sb = (rb - ratio * ra) / (pc - ratio * pb)
            for v in range(v0, 8):
                ca = jnp.broadcast_to(m[v][:, j : j + 1], (8, 128))
                cb = jnp.broadcast_to(m[v][:, j + 1 : j + 2], (8, 128)) - ca * ratio
                if v == v0:
                    ca = jnp.where(sub > r, ca, 0.0)
                    cb = jnp.where(sub > r + 1, cb, 0.0)
                m[v] = m[v] - ca * sa - cb * sb
    for q in range(CAP):
        m = jnp.concatenate(mats[q], axis=0)
        diag = jnp.sum(jnp.where(eye, m, 0.0), axis=1, keepdims=True)
        inv = m[:, 64:] * lax.rsqrt(diag)
        proj = projs[q][:, :64]
        zed = jnp.sum(inv * proj, axis=1, keepdims=True)
        mean_w = jnp.sum(inv * zed, axis=0, keepdims=True)
        trans = inv * (MEMBERS - 1.0) ** 0.5 + mean_w
        trans = trans + (1.0 - jnp.sum(trans, axis=1, keepdims=True)) * (1.0 / MEMBERS)
        trans = trans * coords[8 + q : 9 + q, :64]
        t0 = trans.astype(jnp.bfloat16)
        rest = trans - t0.astype(jnp.float32)
        t1, t2 = split(rest)
        left = jnp.concatenate([t0, t1, t2], axis=0)
        for v in range(2):
            for h in range(2):
                r = q * 4 + v * 2 + h
                x = jnp.concatenate(
                    [wide[c, pl.ds(r, MEMBERS, stride=16), :] for c in range(4)], axis=1
                ).astype(jnp.bfloat16)
                got = jnp.dot(left, x, preferred_element_type=jnp.float32)
                got = got[:64] + (got[64:128] + got[128:])
                for c in range(4):
                    res[h * 4 + c, pl.ds(v * 4 + q, MEMBERS, stride=8), :] = got[
                        :, c * 128 : (c + 1) * 128
                    ]
    for c in range(8):
        body = res[c].reshape(MEMBERS, 2, CAP, 128).astype(jnp.bfloat16)
        out[:, :, :, c * 128 : (c + 1) * 128] = body


def finish(gsum, coords, recv):
    return pl.pallas_call(
        finish_kernel,
        out_shape=jax.ShapeDtypeStruct((MEMBERS, 2, CAP, CELLS), jnp.bfloat16),
        in_specs=[pl.BlockSpec(memory_space=pltpu.VMEM)] * 3,
        out_specs=pl.BlockSpec(memory_space=pltpu.VMEM),
        scratch_shapes=[
            pltpu.VMEM((4, MEMBERS * 16, 128), jnp.float32),
            pltpu.VMEM((8, MEMBERS * 8, 128), jnp.float32),
        ],
        compiler_params=pltpu.CompilerParams(vmem_limit_bytes=VLIM),
        name="finish",
    )(gsum, coords, recv)


def local(prior, location, reading, noise, ocean, holder):
    prior = prior.reshape(2 * TILES, CELLS)
    idx = location.reshape(ROWS, 128)
    read = reading.reshape(ROWS, 128)
    spread = noise.reshape(ROWS, 128)
    gsum, recv, coords = spread_out(
        prior, idx, ocean.reshape(1, TILES), holder.reshape(1, TILES), read, spread
    )
    return finish(gsum, coords, recv)


def solution(mesh):
    in_specs = (
        P("ens", "lev", "tile", None),
        P("lev", "tile"),
        P("lev", "tile"),
        P("lev", "tile"),
        P("tile"),
        P("tile"),
    )
    out_specs = P(None, "lev", ("tile", "ens"), None)
    return jax.shard_map(local, mesh=mesh, in_specs=in_specs, out_specs=out_specs, check_vma=False)
```

```python
import functools
import jax
import jax.numpy as jnp
from jax import lax
from jax.experimental import pallas as pl
from jax.experimental.pallas import tpu as pltpu
from jax.sharding import PartitionSpec as P

TS = 32
CAP = 4
OWNERS = 64
MEMBERS = 64
TILES = 256
CELLS = 1024
STRIPW = 256
ROWS = 48
FIRST_ROW = 112
LENGTH_SQ = (STRIPW / 2.0) ** 2
BLK = 72
EARLY = 8
MESH = pl.DeviceIdType.MESH
VLIM = 56 * 1024 * 1024


def pick_tiles(prior, mask, holder, outg, coords, strip, mine):
    owner = holder[...]
    wet = mask[...] == 1
    key = jnp.where(wet, owner, -1).astype(jnp.float32)
    key_all = jnp.broadcast_to(key, (TILES, TILES))
    key_t = key_all.T
    earlier = lax.broadcasted_iota(jnp.int32, (TILES, TILES), 0) < lax.broadcasted_iota(
        jnp.int32, (TILES, TILES), 1
    )
    same = (key_all == key_t) & earlier
    rank = jnp.sum(jnp.where(same, 1.0, 0.0), axis=0, keepdims=True).astype(jnp.int32)
    slot = jnp.where(wet, owner * CAP + rank, -1)
    tile = lax.broadcasted_iota(jnp.int32, (1, TILES), 1)
    half = (TS - 1) / 2.0
    clat = (tile // 8 * TS).astype(jnp.float32) + half
    clon = (tile % 8 * TS + strip * STRIPW).astype(jnp.float32) + half
    lats, lons, fills = [], [], []
    for q in range(CAP):
        here = slot == mine * CAP + q
        for into, what in ((lats, clat), (lons, clon), (fills, jnp.ones_like(clat))):
            total = jnp.sum(jnp.where(here, what, 0.0), axis=1, keepdims=True)
            into.append(jnp.broadcast_to(total, (1, 128)))
    coords[...] = jnp.concatenate(lats + lons + fills + fills, axis=0)
    rows = lax.broadcasted_iota(jnp.int32, (OWNERS * 16, 2 * TILES), 0)
    total = None
    for h in range(2):
        target = jnp.concatenate([slot * 4 + h, slot * 4 + 2 + h], axis=1)
        target = jnp.where(jnp.concatenate([wet, wet], axis=1), target, -1)
        pick = jnp.where(rows == target, 1.0, 0.0).astype(jnp.bfloat16)
        part = jnp.dot(
            pick, prior[:, h * 512 : (h + 1) * 512], preferred_element_type=jnp.float32
        )
        total = part if total is None else total + part
    outg[...] = total.astype(jnp.bfloat16).reshape(OWNERS, 16, 512)


def one_hot(row):
    line = lax.broadcasted_iota(jnp.int32, (32, 128), 0)
    low = jnp.where(line == (row & 31), 1.0, 0.0).astype(jnp.bfloat16)
    high = jnp.broadcast_to((row >> 5) & 31, (16, 128))
    parts = []
    for a in range(32):
        here = jnp.where(high == a, 1.0, 0.0).astype(jnp.bfloat16)
        parts.append(low * jnp.concatenate([here, here], axis=0))
    return jnp.concatenate(parts, axis=0)


def gather_rows(prior, idx, fvals, first, count, beside):
    def step(j, carry):
        beside(j)
        base = first + j * 8
        pieces, highs = [], []
        for i in range(8):
            row = idx[pl.ds(base + i, 1), :]
            pieces.append(one_hot(row))
            highs.append((row >> 10) - FIRST_ROW)
        onehot = jnp.concatenate(pieces, axis=1)
        high = jnp.concatenate(highs, axis=1)
        got = jnp.dot(prior[FIRST_ROW:, :], onehot, preferred_element_type=jnp.float32)
        line = lax.broadcasted_iota(jnp.int32, got.shape, 0)
        value = jnp.sum(jnp.where(line == high, got, 0.0), axis=0, keepdims=True)
        for i in range(8):
            fvals[pl.ds(base + i, 1), :] = value[:, i * 128 : (i + 1) * 128]
        return carry

    lax.fori_loop(0, count // 8, step, 0)


def weights_into(wscr, idx, noise, tlat, tlon, strip):
    def step(r, carry):
        ids = idx[pl.ds(r, 1), :]
        tile = (ids >> 10) & (TILES - 1)
        cell = ids & (CELLS - 1)
        lat = ((tile >> 3) * TS + (cell >> 5)).astype(jnp.float32)
        lon = (strip * STRIPW + (tile & 7) * TS + (cell & (TS - 1))).astype(jnp.float32)
        dist = (lat - tlat) ** 2 + (lon - tlon) ** 2
        wscr[r] = jnp.exp(-dist / (2.0 * LENGTH_SQ)) * (1.0 / noise[pl.ds(r, 1), :])
        return carry

    lax.fori_loop(0, ROWS, step, 0)


def split(x):
    high = x.astype(jnp.bfloat16)
    low = (x - high.astype(jnp.float32)).astype(jnp.bfloat16)
    return high, low


def gram_steps(fbuf, rows, first, wscr, read, acc, t0, count_t, beside=None):
    count = 8

    def step(k, carry):
        r0 = count * k
        if beside is not None:
            beside(k)
        take = range(count)
        x = jnp.concatenate(
            [fbuf[pl.ds(r0 + i, MEMBERS, stride=rows), :] for i in take], axis=1
        )
        mean = jnp.sum(x, axis=0, keepdims=True) * (1.0 / MEMBERS)
        dev = x - mean
        reading = jnp.concatenate([read[pl.ds(first + r0 + i, 1), :] for i in take], axis=1)
        inno = reading - mean
        w = jnp.concatenate([wscr[first + r0 + i] for i in take], axis=1)
        high, low = split(dev)
        right = jnp.concatenate([high, low], axis=0)
        left = jnp.concatenate(
            [dev * w[t : t + 1, :] for t in range(t0, t0 + count_t)] + [w * inno], axis=0
        )
        lh, ll = split(left)
        dims = (((1,), (1,)), ((), ()))
        acc[...] += lax.dot_general(
            lh, right, dims, preferred_element_type=jnp.float32
        ) + lax.dot_general(ll, right, dims, preferred_element_type=jnp.float32)
        return carry

    lax.fori_loop(0, rows // count, step, 0, unroll=2)


def transforms(gsum, coords, mats, out):
    row = lax.broadcasted_iota(jnp.int32, (MEMBERS, 128), 0)
    lane = lax.broadcasted_iota(jnp.int32, (MEMBERS, 128), 1)
    sub = lax.broadcasted_iota(jnp.int32, (8, 128), 0)
    for q in range(CAP):
        pair = gsum[q // 2, 0:64]
        if q % 2:
            pair = jnp.concatenate([pair[:, 64:], pair[:, :64]], axis=1)
        body = pair + jnp.where(row == lane, MEMBERS - 1.0, 0.0)
        mats[q] = jnp.where(lane < 64, body, jnp.where(row + MEMBERS == lane, 1.0, 0.0))

    def block(b, carry):
        start = pl.multiple_of(b * 8, 8)
        heads = [mats[q, pl.ds(start, 8), :] for q in range(CAP)]
        parts = [[mats[q, 8 * v : 8 * v + 8, :] for v in range(8)] for q in range(CAP)]
        for r in range(0, 8, 2):
            for q in range(CAP):
                ra, rb = heads[q][r : r + 1, :], heads[q][r + 1 : r + 2, :]
                pa = jnp.broadcast_to(ra[:, r : r + 1], (1, 128))
                pb = jnp.broadcast_to(ra[:, r + 1 : r + 2], (1, 128))
                pc = jnp.broadcast_to(rb[:, r + 1 : r + 2], (1, 128))
                inv = 1.0 / pa
                ratio = pb * inv
                sa = ra * inv
                sb = (rb - ratio * ra) / (pc - ratio * pb)

                def reduced(x, rows, pivot):
                    ca = jnp.broadcast_to(x[:, r : r + 1], (8, 128))
                    cb = jnp.broadcast_to(x[:, r + 1 : r + 2], (8, 128)) - ca * ratio
                    ca = jnp.where(rows > pivot, ca, 0.0)
                    cb = jnp.where(rows > pivot + 1, cb, 0.0)
                    return x - ca * sa - cb * sb

                heads[q] = reduced(heads[q], sub, r)
                for v in range(8):
                    parts[q][v] = reduced(parts[q][v], sub + 8 * v, start + r)
        for q in range(CAP):
            for v in range(8):
                mats[q, 8 * v : 8 * v + 8, :] = pltpu.roll(parts[q][v], 120, 1)
        return carry

    lax.fori_loop(0, 8, block, 0)
    for q in range(CAP):
        m = mats[q]
        diag = jnp.sum(jnp.where(row + MEMBERS == lane, m, 0.0), axis=1, keepdims=True)
        inv = m[:, :64] * lax.rsqrt(diag)
        proj = gsum[q // 2, 64:65]
        proj = proj[:, 64:] if q % 2 else proj[:, :64]
        zed = jnp.sum(inv * proj, axis=1, keepdims=True)
        mean_w = jnp.sum(inv * zed, axis=0, keepdims=True)
        trans = inv * (MEMBERS - 1.0) ** 0.5 + mean_w
        trans = trans + (1.0 - jnp.sum(trans, axis=1, keepdims=True)) * (1.0 / MEMBERS)
        out[q] = trans * coords[8 + q : 9 + q, :64]


def main_kernel(
    prior_in, idx_in, mask_in, holder_in, read_in, noise_in, trans, recv,
    prior, idx, mask, holder, read, noise, s_in, outg, vals, fvals, buf_a, buf_b, fa, fb, wscr, cown, cbuf, acc, acc_own, gp, gr, tot, lr,
    tot2, mats, s_own, s_a1, r_a1, s_b1, r_b1, s_a2, r_a2, s_b2, r_b2,
    s_x, r_x, s_c, r_c, s_g, r_g, s_l, r_l,
):
    strips = lax.axis_size("tile")
    strip = lax.axis_index("tile")
    ens = lax.axis_index("ens")
    lev = lax.axis_index("lev")
    y, z = ens % 8, ens // 8
    i1, i2 = y + lev * (z - y), z + lev * (y - z)
    n1, n2 = 1 + 7 * lev, 8 - 7 * lev
    low, high = (strip + strips - 1) % strips, (strip + 1) % strips
    sign = 1 - 2 * lev

    loads = [
        pltpu.make_async_copy(src, dst, s_in.at[i])
        for i, (src, dst) in enumerate(
            (
                (mask_in, mask), (holder_in, holder), (prior_in, prior),
                (idx_in, idx), (read_in, read), (noise_in, noise),
            )
        )
    ]
    for load in loads:
        load.start()
    barrier = pltpu.get_barrier_semaphore()

    def greet(d, carry):
        pl.semaphore_signal(
            barrier, inc=1, device_id={"ens": (ens + d) % OWNERS}, device_id_type=MESH
        )
        return carry

    lax.fori_loop(1, OWNERS, greet, 0)
    for where in ({"tile": low}, {"tile": high}, {"lev": 1 - lev}):
        pl.semaphore_signal(barrier, inc=1, device_id=where, device_id_type=MESH)

    for load in loads:
        load.wait()
    pick_tiles(prior, mask, holder, outg, cown, strip, ens)
    pl.semaphore_wait(barrier, OWNERS - 1 + 3)

    def send(src, dst, ss, rs, where):
        pltpu.make_async_remote_copy(
            src_ref=src, dst_ref=dst, send_sem=ss, recv_sem=rs, device_id=where,
            device_id_type=MESH,
        ).start()

    def wait_for(ref, sem):
        pltpu.make_async_copy(ref, ref, sem).wait()

    def to(dy, dz):
        other = (y + sign * dy + 16) % 8 + 8 * ((z + sign * dz + 16) % 8)
        send(outg.at[other], recv.at[ens], s_x, r_x, {"ens": other})

    def turn(k, carry):
        u, v = 1 + k // 4, k % 4
        to(u, v)
        to(-v, u)
        to(-u, -v)
        to(v, -u)
        return carry

    own_x = pltpu.make_async_copy(outg.at[ens], recv.at[ens], s_own.at[2])
    own_x.start()
    send(cown, cbuf.at[1], s_c.at[0], r_c.at[1], {"tile": low})
    send(cown, cbuf.at[0], s_c.at[1], r_c.at[0], {"tile": high})

    own_a = pltpu.make_async_copy(vals.at[pl.ds(0, 32)], buf_a.at[i2, i1], s_own.at[0])
    own_b = pltpu.make_async_copy(vals.at[pl.ds(32, 16)], buf_b.at[i1, i2], s_own.at[1])

    def first_a(d, carry):
        p = (i1 + d) % 8
        send(vals.at[pl.ds(0, 32)], buf_a.at[i2, i1], s_a1, r_a1, {"ens": p * n1 + i2 * n2})
        return carry

    def first_b(d, carry):
        p = (i2 + d) % 8
        send(vals.at[pl.ds(32, 16)], buf_b.at[i1, i2], s_b1, r_b1, {"ens": i1 * n1 + p * n2})
        return carry

    def along(i, j, ni, nj):
        return {"ens": i * ni + j * nj}

    def second(buf, i, j, ni, nj, ss, rs):
        for d in (4, 3, 5, 2, 6, 1, 7):
            send(buf.at[j], buf.at[j], ss, rs, along(i, (j + d) % 8, ni, nj))

    side_a = (buf_a, i1, i2, n1, n2)
    side_b = (buf_b, i2, i1, n2, n1)

    gather_rows(prior, idx, fvals, 32, 16, lambda j: (turn(2 * j, 0), turn(2 * j + 1, 0)))
    vals[32:48] = fvals[32:48].astype(jnp.bfloat16)
    own_b.start()
    lax.fori_loop(1, 8, first_b, 0)
    gather_rows(prior, idx, fvals, 0, 32, lambda j: turn(4 + j, 0))
    vals[0:32] = fvals[0:32].astype(jnp.bfloat16)
    own_a.start()
    lax.fori_loop(1, 8, first_a, 0)
    own_b.wait()
    wait_for(buf_b.at[0, pl.ds(0, 7)], r_b1)
    second(*side_b, s_b2, r_b2)

    wait_for(cbuf.at[0], r_c.at[0])
    wait_for(cbuf.at[1], r_c.at[1])
    pad = jnp.zeros((4, 128), jnp.float32)
    tlat = jnp.concatenate([cbuf[0, 0:4], cbuf[1, 0:4], cown[0:4], pad], axis=0)
    tlon = jnp.concatenate([cbuf[0, 4:8], cbuf[1, 4:8], cown[4:8], pad], axis=0)
    weights_into(wscr, idx, noise, tlat, tlon, strip)
    acc[...] = jnp.zeros_like(acc)
    acc_own[...] = jnp.zeros_like(acc_own)

    own_a.wait()
    wait_for(buf_a.at[0, pl.ds(0, 7)], r_a1)
    second(*side_a, s_a2, r_a2)

    wait_for(buf_b.at[pl.ds(0, 7)], r_b2)

    def widen_b(k, carry):
        a, b = k // 8, k % 8
        m = a * n1 + b * n2
        fb[pl.ds(pl.multiple_of(m * 16, 16), 16), :] = buf_b[a, b].astype(jnp.float32)
        return carry

    lax.fori_loop(0, MEMBERS, widen_b, 0)

    def some(k):
        turn(8 + 2 * k, 0)
        turn(9 + 2 * k, 0)
        turn(13 + k, 0)

    gram_steps(fb, 16, 32, wscr, read, acc, 0, 8, some)
    turn(15, 0)
    to(4, 4)
    to(4, 0)
    to(0, 4)

    gram_steps(fb, 16, 32, wscr, read, acc_own, 8, 4)

    wait_for(buf_a.at[pl.ds(0, 7)], r_a2)

    def widen_a(k, carry):
        a, b = k // 8, k % 8
        m = b * n1 + a * n2
        fa[pl.ds(pl.multiple_of(m * 32, 32), 32), :] = buf_a[a, b].astype(jnp.float32)
        return carry

    lax.fori_loop(0, MEMBERS, widen_a, 0)
    gram_steps(fa, 32, 0, wscr, read, acc, 0, 8)

    def pack(src, rows, first, count, dst):
        for p in range(2):
            sides, tails = [], []
            for q in range(2):
                t = first + p * 2 + q
                block = src[t * MEMBERS : (t + 1) * MEMBERS, :]
                sides.append(block[:, :64] + block[:, 64:])
                at = count * MEMBERS + rows + p * 2 + q
                line = src[at : at + 1, :]
                tails.append(line[:, :64] + line[:, 64:])
            dst[p, 0:64] = jnp.concatenate(sides, axis=1)
            dst[p, 64:BLK] = jnp.broadcast_to(jnp.concatenate(tails, axis=1), (8, 128))

    pack(acc, 0, 0, 8, gp.at[0])
    send(gp.at[0], gr.at[1], s_g.at[0], r_g.at[1], {"tile": low})
    pack(acc, 4, 4, 8, gp.at[1])
    send(gp.at[1], gr.at[0], s_g.at[1], r_g.at[0], {"tile": high})
    gram_steps(fa, 32, 0, wscr, read, acc_own, 8, 4)
    pack(acc_own, 8, 0, 4, gp.at[2])
    wait_for(gr.at[0], r_g.at[0])
    wait_for(gr.at[1], r_g.at[1])
    tot[...] = (
        gp[2]
        + jnp.where(strip > 0, gr[0], jnp.zeros_like(gr[0]))
        + jnp.where(strip < strips - 1, gr[1], jnp.zeros_like(gr[1]))
    )
    send(tot, lr, s_l, r_l, {"lev": 1 - lev})
    wait_for(lr, r_l)
    tot2[...] = tot[...] + lr[...]
    transforms(tot2, cown, mats, trans)

    own_x.wait()
    wait_for(recv.at[pl.ds(0, OWNERS - 1)], r_x)
    wait_for(outg.at[pl.ds(0, OWNERS - 1)], s_x)
    wait_for(buf_a.at[0, pl.ds(0, 7)], s_a1)
    wait_for(buf_b.at[0, pl.ds(0, 7)], s_b1)
    wait_for(buf_a.at[pl.ds(0, 7)], s_a2)
    wait_for(buf_b.at[pl.ds(0, 7)], s_b2)
    for i in range(2):
        wait_for(cown, s_c.at[i])
        wait_for(gp.at[0], s_g.at[i])
    wait_for(tot, s_l)


def spread_out(prior, idx, mask, holder, read, noise):
    dma = pltpu.SemaphoreType.DMA
    vmem = pl.BlockSpec(memory_space=pltpu.VMEM)
    any_ = pl.BlockSpec(memory_space=pl.ANY)
    return pl.pallas_call(
        main_kernel,
        out_shape=(
            jax.ShapeDtypeStruct((CAP, MEMBERS, MEMBERS), jnp.float32),
            jax.ShapeDtypeStruct((MEMBERS, 16, 512), jnp.bfloat16),
        ),
        in_specs=[any_] * 6,
        out_specs=[vmem, any_],
        scratch_shapes=[
            pltpu.VMEM((2 * TILES, CELLS), jnp.bfloat16),
            pltpu.VMEM((ROWS, 128), jnp.int32),
            pltpu.VMEM((1, TILES), jnp.int32),
            pltpu.VMEM((1, TILES), jnp.int32),
            pltpu.VMEM((ROWS, 128), jnp.float32),
            pltpu.VMEM((ROWS, 128), jnp.float32),
            dma((6,)),
            pltpu.VMEM((OWNERS, 16, 512), jnp.bfloat16),
            pltpu.VMEM((ROWS, 128), jnp.bfloat16),
            pltpu.VMEM((ROWS, 128), jnp.float32),
            pltpu.VMEM((8, 8, 32, 128), jnp.bfloat16),
            pltpu.VMEM((8, 8, 16, 128), jnp.bfloat16),
            pltpu.VMEM((MEMBERS * 32, 128), jnp.float32),
            pltpu.VMEM((MEMBERS * 16, 128), jnp.float32),
            pltpu.VMEM((ROWS, 16, 128), jnp.float32),
            pltpu.VMEM((16, 128), jnp.float32),
            pltpu.VMEM((2, 16, 128), jnp.float32),
            pltpu.VMEM((8 * MEMBERS + 16, 128), jnp.float32),
            pltpu.VMEM((4 * MEMBERS + 16, 128), jnp.float32),
            pltpu.VMEM((3, 2, BLK, 128), jnp.float32),
            pltpu.VMEM((2, 2, BLK, 128), jnp.float32),
            pltpu.VMEM((2, BLK, 128), jnp.float32),
            pltpu.VMEM((2, BLK, 128), jnp.float32),
            pltpu.VMEM((2, BLK, 128), jnp.float32),
            pltpu.VMEM((CAP, MEMBERS, 128), jnp.float32),
            dma((3,)),
            dma, dma, dma, dma, dma, dma, dma, dma,
            dma, dma,
            dma((2,)), dma((2,)), dma((2,)), dma((2,)),
            dma, dma,
        ],
        compiler_params=pltpu.CompilerParams(
            collective_id=1, has_side_effects=True, vmem_limit_bytes=VLIM
        ),
        name="spread",
    )(prior, idx, mask, holder, read, noise)


def finish_kernel(trans, recv, out, wide, res):
    for c in range(4):
        wide[c] = recv[:, :, c * 128 : (c + 1) * 128].astype(jnp.float32).reshape(-1, 128)
    for q in range(CAP):
        t0 = trans[q].astype(jnp.bfloat16)
        rest = trans[q] - t0.astype(jnp.float32)
        t1, t2 = split(rest)
        left = jnp.concatenate([t0, t1, t2], axis=0)
        for v in range(2):
            for h in range(2):
                r = q * 4 + v * 2 + h
                x = jnp.concatenate(
                    [wide[c, pl.ds(r, MEMBERS, stride=16), :] for c in range(4)], axis=1
                ).astype(jnp.bfloat16)
                got = jnp.dot(left, x, preferred_element_type=jnp.float32)
                got = got[:64] + (got[64:128] + got[128:])
                for c in range(4):
                    res[h * 4 + c, pl.ds(v * 4 + q, MEMBERS, stride=8), :] = got[
                        :, c * 128 : (c + 1) * 128
                    ]
    for c in range(8):
        body = res[c].reshape(MEMBERS, 2, CAP, 128).astype(jnp.bfloat16)
        out[:, :, :, c * 128 : (c + 1) * 128] = body


def finish(trans, recv):
    return pl.pallas_call(
        finish_kernel,
        out_shape=jax.ShapeDtypeStruct((MEMBERS, 2, CAP, CELLS), jnp.bfloat16),
        in_specs=[pl.BlockSpec(memory_space=pltpu.VMEM)] * 2,
        out_specs=pl.BlockSpec(memory_space=pltpu.VMEM),
        scratch_shapes=[
            pltpu.VMEM((4, MEMBERS * 16, 128), jnp.float32),
            pltpu.VMEM((8, MEMBERS * 8, 128), jnp.float32),
        ],
        compiler_params=pltpu.CompilerParams(vmem_limit_bytes=VLIM),
        name="finish",
    )(trans, recv)


def local(prior, location, reading, noise, ocean, holder):
    prior = prior.reshape(2 * TILES, CELLS)
    idx = location.reshape(ROWS, 128)
    read = reading.reshape(ROWS, 128)
    spread = noise.reshape(ROWS, 128)
    trans, recv = spread_out(
        prior, idx, ocean.reshape(1, TILES), holder.reshape(1, TILES), read, spread
    )
    return finish(trans, recv)


def solution(mesh):
    in_specs = (
        P("ens", "lev", "tile", None),
        P("lev", "tile"),
        P("lev", "tile"),
        P("lev", "tile"),
        P("tile"),
        P("tile"),
    )
    out_specs = P(None, "lev", ("tile", "ens"), None)
    return jax.shard_map(local, mesh=mesh, in_specs=in_specs, out_specs=out_specs, check_vma=False)
```

```python
import functools
import jax
import jax.numpy as jnp
from jax import lax
from jax.experimental import pallas as pl
from jax.experimental.pallas import tpu as pltpu
from jax.sharding import PartitionSpec as P

TS = 32
CAP = 4
OWNERS = 64
MEMBERS = 64
TILES = 256
CELLS = 1024
STRIPW = 256
ROWS = 48
FIRST_ROW = 112
LENGTH_SQ = (STRIPW / 2.0) ** 2
BLK = 72
EARLY = 8
MESH = pl.DeviceIdType.MESH
VLIM = 56 * 1024 * 1024


def pick_tiles(prior, mask, holder, outg, coords, strip, mine):
    owner = holder[...]
    wet = mask[...] == 1
    key = jnp.where(wet, owner, -1).astype(jnp.float32)
    key_all = jnp.broadcast_to(key, (TILES, TILES))
    key_t = key_all.T
    earlier = lax.broadcasted_iota(jnp.int32, (TILES, TILES), 0) < lax.broadcasted_iota(
        jnp.int32, (TILES, TILES), 1
    )
    same = (key_all == key_t) & earlier
    rank = jnp.sum(jnp.where(same, 1.0, 0.0), axis=0, keepdims=True).astype(jnp.int32)
    slot = jnp.where(wet, owner * CAP + rank, -1)
    tile = lax.broadcasted_iota(jnp.int32, (1, TILES), 1)
    half = (TS - 1) / 2.0
    clat = (tile // 8 * TS).astype(jnp.float32) + half
    clon = (tile % 8 * TS + strip * STRIPW).astype(jnp.float32) + half
    lats, lons, fills = [], [], []
    for q in range(CAP):
        here = slot == mine * CAP + q
        for into, what in ((lats, clat), (lons, clon), (fills, jnp.ones_like(clat))):
            total = jnp.sum(jnp.where(here, what, 0.0), axis=1, keepdims=True)
            into.append(jnp.broadcast_to(total, (1, 128)))
    coords[...] = jnp.concatenate(lats + lons + fills + fills, axis=0)
    rows = lax.broadcasted_iota(jnp.int32, (OWNERS * 16, 2 * TILES), 0)
    total = None
    for h in range(2):
        target = jnp.concatenate([slot * 4 + h, slot * 4 + 2 + h], axis=1)
        target = jnp.where(jnp.concatenate([wet, wet], axis=1), target, -1)
        pick = jnp.where(rows == target, 1.0, 0.0).astype(jnp.bfloat16)
        part = jnp.dot(
            pick, prior[:, h * 512 : (h + 1) * 512], preferred_element_type=jnp.float32
        )
        total = part if total is None else total + part
    outg[...] = total.astype(jnp.bfloat16).reshape(OWNERS, 16, 512)


def one_hot(row):
    line = lax.broadcasted_iota(jnp.int32, (32, 128), 0)
    low = jnp.where(line == (row & 31), 1.0, 0.0).astype(jnp.bfloat16)
    high = jnp.broadcast_to((row >> 5) & 31, (16, 128))
    parts = []
    for a in range(32):
        here = jnp.where(high == a, 1.0, 0.0).astype(jnp.bfloat16)
        parts.append(low * jnp.concatenate([here, here], axis=0))
    return jnp.concatenate(parts, axis=0)


def gather_rows(prior, idx, fvals, first, count, beside):
    def step(j, carry):
        beside(j)
        base = first + j * 8
        pieces, highs = [], []
        for i in range(8):
            row = idx[pl.ds(base + i, 1), :]
            pieces.append(one_hot(row))
            highs.append((row >> 10) - FIRST_ROW)
        onehot = jnp.concatenate(pieces, axis=1)
        high = jnp.concatenate(highs, axis=1)
        got = jnp.dot(prior[FIRST_ROW:, :], onehot, preferred_element_type=jnp.float32)
        line = lax.broadcasted_iota(jnp.int32, got.shape, 0)
        value = jnp.sum(jnp.where(line == high, got, 0.0), axis=0, keepdims=True)
        for i in range(8):
            fvals[pl.ds(base + i, 1), :] = value[:, i * 128 : (i + 1) * 128]
        return carry

    lax.fori_loop(0, count // 8, step, 0)


def weights_into(wscr, idx, noise, tlat, tlon, strip):
    def step(r, carry):
        ids = idx[pl.ds(r, 1), :]
        tile = (ids >> 10) & (TILES - 1)
        cell = ids & (CELLS - 1)
        lat = ((tile >> 3) * TS + (cell >> 5)).astype(jnp.float32)
        lon = (strip * STRIPW + (tile & 7) * TS + (cell & (TS - 1))).astype(jnp.float32)
        dist = (lat - tlat) ** 2 + (lon - tlon) ** 2
        wscr[r] = jnp.exp(-dist / (2.0 * LENGTH_SQ)) * (1.0 / noise[pl.ds(r, 1), :])
        return carry

    lax.fori_loop(0, ROWS, step, 0, unroll=4)


def split(x):
    high = x.astype(jnp.bfloat16)
    low = (x - high.astype(jnp.float32)).astype(jnp.bfloat16)
    return high, low


def gram_steps(fbuf, rows, first, wscr, read, acc, t0, count_t, beside=None):
    count = 8

    def step(k, carry):
        r0 = count * k
        if beside is not None:
            beside(k)
        take = range(count)
        x = jnp.concatenate(
            [fbuf[pl.ds(r0 + i, MEMBERS, stride=rows), :] for i in take], axis=1
        )
        mean = jnp.sum(x, axis=0, keepdims=True) * (1.0 / MEMBERS)
        dev = x - mean
        reading = jnp.concatenate([read[pl.ds(first + r0 + i, 1), :] for i in take], axis=1)
        inno = reading - mean
        w = jnp.concatenate([wscr[first + r0 + i] for i in take], axis=1)
        high, low = split(dev)
        right = jnp.concatenate([high, low], axis=0)
        left = jnp.concatenate(
            [dev * w[t : t + 1, :] for t in range(t0, t0 + count_t)] + [w * inno], axis=0
        )
        lh, ll = split(left)
        dims = (((1,), (1,)), ((), ()))
        acc[...] += lax.dot_general(
            lh, right, dims, preferred_element_type=jnp.float32
        ) + lax.dot_general(ll, right, dims, preferred_element_type=jnp.float32)
        return carry

    lax.fori_loop(0, rows // count, step, 0, unroll=2)


def transforms(gsum, coords, mats, out):
    row = lax.broadcasted_iota(jnp.int32, (MEMBERS, 128), 0)
    lane = lax.broadcasted_iota(jnp.int32, (MEMBERS, 128), 1)
    sub = lax.broadcasted_iota(jnp.int32, (8, 128), 0)
    for q in range(CAP):
        pair = gsum[q // 2, 0:64]
        if q % 2:
            pair = jnp.concatenate([pair[:, 64:], pair[:, :64]], axis=1)
        body = pair + jnp.where(row == lane, MEMBERS - 1.0, 0.0)
        mats[q] = jnp.where(lane < 64, body, jnp.where(row + MEMBERS == lane, 1.0, 0.0))

    def block(b, carry):
        start = pl.multiple_of(b * 8, 8)
        heads = [mats[q, pl.ds(start, 8), :] for q in range(CAP)]
        parts = [[mats[q, 8 * v : 8 * v + 8, :] for v in range(8)] for q in range(CAP)]
        for r in range(0, 8, 2):
            for q in range(CAP):
                ra, rb = heads[q][r : r + 1, :], heads[q][r + 1 : r + 2, :]
                pa = jnp.broadcast_to(ra[:, r : r + 1], (1, 128))
                pb = jnp.broadcast_to(ra[:, r + 1 : r + 2], (1, 128))
                pc = jnp.broadcast_to(rb[:, r + 1 : r + 2], (1, 128))
                inv = 1.0 / pa
                ratio = pb * inv
                sa = ra * inv
                sb = (rb - ratio * ra) / (pc - ratio * pb)

                def reduced(x, rows, pivot):
                    ca = jnp.broadcast_to(x[:, r : r + 1], (8, 128))
                    cb = jnp.broadcast_to(x[:, r + 1 : r + 2], (8, 128)) - ca * ratio
                    ca = jnp.where(rows > pivot, ca, 0.0)
                    cb = jnp.where(rows > pivot + 1, cb, 0.0)
                    return x - ca * sa - cb * sb

                heads[q] = reduced(heads[q], sub, r)
                for v in range(8):
                    parts[q][v] = reduced(parts[q][v], sub + 8 * v, start + r)
        for q in range(CAP):
            for v in range(8):
                mats[q, 8 * v : 8 * v + 8, :] = pltpu.roll(parts[q][v], 120, 1)
        return carry

    lax.fori_loop(0, 8, block, 0)
    for q in range(CAP):
        m = mats[q]
        diag = jnp.sum(jnp.where(row + MEMBERS == lane, m, 0.0), axis=1, keepdims=True)
        inv = m[:, :64] * lax.rsqrt(diag)
        proj = gsum[q // 2, 64:65]
        proj = proj[:, 64:] if q % 2 else proj[:, :64]
        zed = jnp.sum(inv * proj, axis=1, keepdims=True)
        mean_w = jnp.sum(inv * zed, axis=0, keepdims=True)
        trans = inv * (MEMBERS - 1.0) ** 0.5 + mean_w
        trans = trans + (1.0 - jnp.sum(trans, axis=1, keepdims=True)) * (1.0 / MEMBERS)
        out[q] = trans * coords[8 + q : 9 + q, :64]


def main_kernel(
    prior_in, idx_in, mask_in, holder_in, read_in, noise_in, trans, recv,
    prior, idx, mask, holder, read, noise, s_in, outg, vals, fvals, buf_a, buf_b, fa, fb, wscr, cown, cbuf, acc, acc_own, gp, gr, tot, lr,
    tot2, mats, s_own, s_a1, r_a1, s_b1, r_b1, s_a2, r_a2, s_b2, r_b2,
    s_x, r_x, s_c, r_c, s_g, r_g, s_l, r_l,
):
    strips = lax.axis_size("tile")
    strip = lax.axis_index("tile")
    ens = lax.axis_index("ens")
    lev = lax.axis_index("lev")
    y, z = ens % 8, ens // 8
    i1, i2 = y + lev * (z - y), z + lev * (y - z)
    n1, n2 = 1 + 7 * lev, 8 - 7 * lev
    low, high = (strip + strips - 1) % strips, (strip + 1) % strips
    sign = 1 - 2 * lev

    loads = [
        pltpu.make_async_copy(src, dst, s_in.at[i])
        for i, (src, dst) in enumerate(
            (
                (mask_in, mask), (holder_in, holder), (prior_in, prior),
                (idx_in, idx), (read_in, read), (noise_in, noise),
            )
        )
    ]
    for load in loads:
        load.start()
    barrier = pltpu.get_barrier_semaphore()

    def greet(d, carry):
        pl.semaphore_signal(
            barrier, inc=1, device_id={"ens": (ens + d) % OWNERS}, device_id_type=MESH
        )
        return carry

    lax.fori_loop(1, OWNERS, greet, 0)
    for where in ({"tile": low}, {"tile": high}, {"lev": 1 - lev}):
        pl.semaphore_signal(barrier, inc=1, device_id=where, device_id_type=MESH)

    for load in loads:
        load.wait()
    pick_tiles(prior, mask, holder, outg, cown, strip, ens)
    pl.semaphore_wait(barrier, OWNERS - 1 + 3)

    def send(src, dst, ss, rs, where):
        pltpu.make_async_remote_copy(
            src_ref=src, dst_ref=dst, send_sem=ss, recv_sem=rs, device_id=where,
            device_id_type=MESH,
        ).start()

    def wait_for(ref, sem):
        pltpu.make_async_copy(ref, ref, sem).wait()

    def to(dy, dz):
        other = (y + sign * dy + 16) % 8 + 8 * ((z + sign * dz + 16) % 8)
        send(outg.at[other], recv.at[ens], s_x, r_x, {"ens": other})

    def turn(k, carry):
        u, v = 1 + k // 4, k % 4
        to(u, v)
        to(-v, u)
        to(-u, -v)
        to(v, -u)
        return carry

    own_x = pltpu.make_async_copy(outg.at[ens], recv.at[ens], s_own.at[2])
    own_x.start()
    send(cown, cbuf.at[1], s_c.at[0], r_c.at[1], {"tile": low})
    send(cown, cbuf.at[0], s_c.at[1], r_c.at[0], {"tile": high})

    own_a = pltpu.make_async_copy(vals.at[pl.ds(0, 32)], buf_a.at[i2, i1], s_own.at[0])
    own_b = pltpu.make_async_copy(vals.at[pl.ds(32, 16)], buf_b.at[i1, i2], s_own.at[1])

    def first_a(d, carry):
        p = (i1 + d) % 8
        send(vals.at[pl.ds(0, 32)], buf_a.at[i2, i1], s_a1, r_a1, {"ens": p * n1 + i2 * n2})
        return carry

    def first_b(d, carry):
        p = (i2 + d) % 8
        send(vals.at[pl.ds(32, 16)], buf_b.at[i1, i2], s_b1, r_b1, {"ens": i1 * n1 + p * n2})
        return carry

    def along(i, j, ni, nj):
        return {"ens": i * ni + j * nj}

    def second(buf, i, j, ni, nj, ss, rs):
        for d in (4, 3, 5, 2, 6, 1, 7):
            send(buf.at[j], buf.at[j], ss, rs, along(i, (j + d) % 8, ni, nj))

    side_a = (buf_a, i1, i2, n1, n2)
    side_b = (buf_b, i2, i1, n2, n1)

    gather_rows(prior, idx, fvals, 32, 16, lambda j: (turn(2 * j, 0), turn(2 * j + 1, 0)))
    vals[32:48] = fvals[32:48].astype(jnp.bfloat16)
    own_b.start()
    lax.fori_loop(1, 8, first_b, 0)
    gather_rows(prior, idx, fvals, 0, 32, lambda j: turn(4 + j, 0))
    vals[0:32] = fvals[0:32].astype(jnp.bfloat16)
    own_a.start()
    lax.fori_loop(1, 8, first_a, 0)
    own_b.wait()
    wait_for(buf_b.at[0, pl.ds(0, 7)], r_b1)
    second(*side_b, s_b2, r_b2)

    wait_for(cbuf.at[0], r_c.at[0])
    wait_for(cbuf.at[1], r_c.at[1])
    pad = jnp.zeros((4, 128), jnp.float32)
    tlat = jnp.concatenate([cbuf[0, 0:4], cbuf[1, 0:4], cown[0:4], pad], axis=0)
    tlon = jnp.concatenate([cbuf[0, 4:8], cbuf[1, 4:8], cown[4:8], pad], axis=0)
    weights_into(wscr, idx, noise, tlat, tlon, strip)
    acc[...] = jnp.zeros_like(acc)
    acc_own[...] = jnp.zeros_like(acc_own)

    own_a.wait()
    wait_for(buf_a.at[0, pl.ds(0, 7)], r_a1)
    second(*side_a, s_a2, r_a2)

    wait_for(buf_b.at[pl.ds(0, 7)], r_b2)

    def widen_b(k, carry):
        a, b = k // 8, k % 8
        m = a * n1 + b * n2
        fb[pl.ds(pl.multiple_of(m * 16, 16), 16), :] = buf_b[a, b].astype(jnp.float32)
        return carry

    lax.fori_loop(0, MEMBERS, widen_b, 0, unroll=8)

    def some(k):
        turn(8 + 2 * k, 0)
        turn(9 + 2 * k, 0)
        turn(13 + k, 0)

    gram_steps(fb, 16, 32, wscr, read, acc, 0, 8, some)
    turn(15, 0)
    to(4, 4)
    to(4, 0)
    to(0, 4)

    gram_steps(fb, 16, 32, wscr, read, acc_own, 8, 4)

    wait_for(buf_a.at[pl.ds(0, 7)], r_a2)

    def widen_a(k, carry):
        a, b = k // 8, k % 8
        m = b * n1 + a * n2
        fa[pl.ds(pl.multiple_of(m * 32, 32), 32), :] = buf_a[a, b].astype(jnp.float32)
        return carry

    lax.fori_loop(0, MEMBERS, widen_a, 0, unroll=8)
    gram_steps(fa, 32, 0, wscr, read, acc, 0, 8)

    def pack(src, rows, first, count, dst):
        for p in range(2):
            sides, tails = [], []
            for q in range(2):
                t = first + p * 2 + q
                block = src[t * MEMBERS : (t + 1) * MEMBERS, :]
                sides.append(block[:, :64] + block[:, 64:])
                at = count * MEMBERS + rows + p * 2 + q
                line = src[at : at + 1, :]
                tails.append(line[:, :64] + line[:, 64:])
            dst[p, 0:64] = jnp.concatenate(sides, axis=1)
            dst[p, 64:BLK] = jnp.broadcast_to(jnp.concatenate(tails, axis=1), (8, 128))

    pack(acc, 0, 0, 8, gp.at[0])
    send(gp.at[0], gr.at[1], s_g.at[0], r_g.at[1], {"tile": low})
    pack(acc, 4, 4, 8, gp.at[1])
    send(gp.at[1], gr.at[0], s_g.at[1], r_g.at[0], {"tile": high})
    gram_steps(fa, 32, 0, wscr, read, acc_own, 8, 4)
    pack(acc_own, 8, 0, 4, gp.at[2])
    wait_for(gr.at[0], r_g.at[0])
    wait_for(gr.at[1], r_g.at[1])
    tot[...] = (
        gp[2]
        + jnp.where(strip > 0, gr[0], jnp.zeros_like(gr[0]))
        + jnp.where(strip < strips - 1, gr[1], jnp.zeros_like(gr[1]))
    )
    send(tot, lr, s_l, r_l, {"lev": 1 - lev})
    wait_for(lr, r_l)
    tot2[...] = tot[...] + lr[...]
    transforms(tot2, cown, mats, trans)

    own_x.wait()
    wait_for(recv.at[pl.ds(0, OWNERS - 1)], r_x)
    wait_for(outg.at[pl.ds(0, OWNERS - 1)], s_x)
    wait_for(buf_a.at[0, pl.ds(0, 7)], s_a1)
    wait_for(buf_b.at[0, pl.ds(0, 7)], s_b1)
    wait_for(buf_a.at[pl.ds(0, 7)], s_a2)
    wait_for(buf_b.at[pl.ds(0, 7)], s_b2)
    for i in range(2):
        wait_for(cown, s_c.at[i])
        wait_for(gp.at[0], s_g.at[i])
    wait_for(tot, s_l)


def spread_out(prior, idx, mask, holder, read, noise):
    dma = pltpu.SemaphoreType.DMA
    vmem = pl.BlockSpec(memory_space=pltpu.VMEM)
    any_ = pl.BlockSpec(memory_space=pl.ANY)
    return pl.pallas_call(
        main_kernel,
        out_shape=(
            jax.ShapeDtypeStruct((CAP, MEMBERS, MEMBERS), jnp.float32),
            jax.ShapeDtypeStruct((MEMBERS, 16, 512), jnp.bfloat16),
        ),
        in_specs=[any_] * 6,
        out_specs=[vmem, any_],
        scratch_shapes=[
            pltpu.VMEM((2 * TILES, CELLS), jnp.bfloat16),
            pltpu.VMEM((ROWS, 128), jnp.int32),
            pltpu.VMEM((1, TILES), jnp.int32),
            pltpu.VMEM((1, TILES), jnp.int32),
            pltpu.VMEM((ROWS, 128), jnp.float32),
            pltpu.VMEM((ROWS, 128), jnp.float32),
            dma((6,)),
            pltpu.VMEM((OWNERS, 16, 512), jnp.bfloat16),
            pltpu.VMEM((ROWS, 128), jnp.bfloat16),
            pltpu.VMEM((ROWS, 128), jnp.float32),
            pltpu.VMEM((8, 8, 32, 128), jnp.bfloat16),
            pltpu.VMEM((8, 8, 16, 128), jnp.bfloat16),
            pltpu.VMEM((MEMBERS * 32, 128), jnp.float32),
            pltpu.VMEM((MEMBERS * 16, 128), jnp.float32),
            pltpu.VMEM((ROWS, 16, 128), jnp.float32),
            pltpu.VMEM((16, 128), jnp.float32),
            pltpu.VMEM((2, 16, 128), jnp.float32),
            pltpu.VMEM((8 * MEMBERS + 16, 128), jnp.float32),
            pltpu.VMEM((4 * MEMBERS + 16, 128), jnp.float32),
            pltpu.VMEM((3, 2, BLK, 128), jnp.float32),
            pltpu.VMEM((2, 2, BLK, 128), jnp.float32),
            pltpu.VMEM((2, BLK, 128), jnp.float32),
            pltpu.VMEM((2, BLK, 128), jnp.float32),
            pltpu.VMEM((2, BLK, 128), jnp.float32),
            pltpu.VMEM((CAP, MEMBERS, 128), jnp.float32),
            dma((3,)),
            dma, dma, dma, dma, dma, dma, dma, dma,
            dma, dma,
            dma((2,)), dma((2,)), dma((2,)), dma((2,)),
            dma, dma,
        ],
        compiler_params=pltpu.CompilerParams(
            collective_id=1, has_side_effects=True, vmem_limit_bytes=VLIM
        ),
        name="spread",
    )(prior, idx, mask, holder, read, noise)


def finish_kernel(trans, recv, out, wide, res):
    for c in range(4):
        wide[c] = recv[:, :, c * 128 : (c + 1) * 128].astype(jnp.float32).reshape(-1, 128)
    for q in range(CAP):
        t0 = trans[q].astype(jnp.bfloat16)
        rest = trans[q] - t0.astype(jnp.float32)
        t1, t2 = split(rest)
        left = jnp.concatenate([t0, t1, t2], axis=0)
        for v in range(2):
            for h in range(2):
                r = q * 4 + v * 2 + h
                x = jnp.concatenate(
                    [wide[c, pl.ds(r, MEMBERS, stride=16), :] for c in range(4)], axis=1
                ).astype(jnp.bfloat16)
                got = jnp.dot(left, x, preferred_element_type=jnp.float32)
                got = got[:64] + (got[64:128] + got[128:])
                for c in range(4):
                    res[h * 4 + c, pl.ds(v * 4 + q, MEMBERS, stride=8), :] = got[
                        :, c * 128 : (c + 1) * 128
                    ]
    for c in range(8):
        body = res[c].reshape(MEMBERS, 2, CAP, 128).astype(jnp.bfloat16)
        out[:, :, :, c * 128 : (c + 1) * 128] = body


def finish(trans, recv):
    return pl.pallas_call(
        finish_kernel,
        out_shape=jax.ShapeDtypeStruct((MEMBERS, 2, CAP, CELLS), jnp.bfloat16),
        in_specs=[pl.BlockSpec(memory_space=pltpu.VMEM)] * 2,
        out_specs=pl.BlockSpec(memory_space=pltpu.VMEM),
        scratch_shapes=[
            pltpu.VMEM((4, MEMBERS * 16, 128), jnp.float32),
            pltpu.VMEM((8, MEMBERS * 8, 128), jnp.float32),
        ],
        compiler_params=pltpu.CompilerParams(vmem_limit_bytes=VLIM),
        name="finish",
    )(trans, recv)


def local(prior, location, reading, noise, ocean, holder):
    prior = prior.reshape(2 * TILES, CELLS)
    idx = location.reshape(ROWS, 128)
    read = reading.reshape(ROWS, 128)
    spread = noise.reshape(ROWS, 128)
    trans, recv = spread_out(
        prior, idx, ocean.reshape(1, TILES), holder.reshape(1, TILES), read, spread
    )
    return finish(trans, recv)


def solution(mesh):
    in_specs = (
        P("ens", "lev", "tile", None),
        P("lev", "tile"),
        P("lev", "tile"),
        P("lev", "tile"),
        P("tile"),
        P("tile"),
    )
    out_specs = P(None, "lev", ("tile", "ens"), None)
    return jax.shard_map(local, mesh=mesh, in_specs=in_specs, out_specs=out_specs, check_vma=False)
```
